32 devices in a mesh: prompt: 4 (over y, x), resp: 8 (over z, core).
Axes of the slice: x: 2, y: 2, z: 4, core: 2. Of those that a mesh axis runs over, the one named last changes fastest.
Arguments:
- query: bfloat16 [32, 256, 2048], P(('prompt', 'resp')), may hold values from -6 to 6
- resp_keys: bfloat16 [32, 256, 512], P(('prompt', 'resp')), may hold values from -6 to 6
- resp_values: bfloat16 [32, 256, 512], P(('prompt', 'resp')), may hold values from -6 to 6
- prompt_keys: bfloat16 [8, 32, 512], P(None, 'prompt'), may hold values from -6 to 6
- prompt_values: bfloat16 [8, 32, 512], P(None, 'prompt'), may hold values from -6 to 6
- out_grad: bfloat16 [32, 256, 2048], P(('prompt', 'resp')), may hold values from -6 to 6
- group: int32 [32], replicated, may hold values from 0 to 7
- lengths: int32 [32], P(('prompt', 'resp')), may hold values from 1 to 256, 5120 in all
Outputs:
- query_grad: bfloat16 [32, 256, 2048], P(('prompt', 'resp'))
- resp_key_grad: bfloat16 [32, 256, 512], P(('prompt', 'resp'))
- resp_value_grad: bfloat16 [32, 256, 512], P(('prompt', 'resp'))
- prompt_key_grad: float32 [8, 32, 512], P(None, 'prompt')
- prompt_value_grad: float32 [8, 32, 512], P(None, 'prompt')
The draws below stay inside these ranges and needn't reach their ends.
Inputs may be any that keep to these rules, and one draw needn't show every extreme that they name: `group`: response r stands on device r of prompt+resp, in the mesh's order. `lengths`: a response's live tokens come first; some response fills all 256 slots.
All inputs are finite; a program needn't handle non-finite values. No bound on the sum of `lengths` on one device may be relied on, other than what follows from the above.
Results may differ from the reference program's by a relative error of at most 0.0097.
Values may be sent and summed in bfloat16 or wider, within the bound.
A program may use at most 64 MiB of HBM per device.

```python
import math
import jax
import jax.numpy as jnp
import numpy as np
from jax import lax

QH = 16
KVH = 4
HD = 128
PROMPTS = 8
RLEN = 256
QW = 2048
KVW = 512
PLEN = 32
RESPONSES = 32


def draw_query(key, part):
    key = jax.random.fold_in(key, 11)
    shape_full = (RESPONSES, RLEN, QH, HD)
    drawn = jnp.clip(jax.random.normal(key, shape_full, jnp.float32), -6.0, 6.0)
    return drawn.reshape(RESPONSES, RLEN, QH * HD).astype(jnp.bfloat16)


def draw_prompt_keys(key, part):
    key = jax.random.fold_in(key, 12)
    shape_full = (PROMPTS, PLEN, KVH, HD)
    drawn = jnp.clip(jax.random.normal(key, shape_full, jnp.float32), -6.0, 6.0)
    return drawn.reshape(PROMPTS, PLEN, KVH * HD).astype(jnp.bfloat16)


def with_ends(values, rng, least, largest):
    longest = values.shape.index(max(values.shape))
    spots = []
    for shift in (0, 1):
        where = [jax.random.randint(jax.random.fold_in(rng, axis), (), 0, length) for axis, length in enumerate(values.shape)]
        where[longest] = (where[longest] + shift) % values.shape[longest]
        spots.append(tuple(where))
    return values.at[spots[0]].set(least).at[spots[1]].set(largest)


def shard_levels(key, extent, cuts, least, high):
    def one(position, shards_of):
        heights = jax.random.uniform(jax.random.fold_in(jax.random.fold_in(key, 6), position), (shards_of,), jnp.float32, least / len(cuts), high / len(cuts))
        return jnp.repeat(jnp.exp(heights), extent[position] // shards_of).reshape((-1,) + (1,) * (len(extent) - position - 1))

    factor_of = one(*cuts[0])
    for cut in cuts[1:]:
        factor_of = factor_of * one(*cut)
    return factor_of


def profile(number_of, total, bound, slope):
    weights = [(1 << 20) // math.isqrt(standing ** slope) + 1 for standing in range(2, number_of + 1)]
    surplus, counts = total - bound - (number_of - 1), [1] * (number_of - 1)
    while surplus > 0:
        movable = [i for i in range(number_of - 1) if counts[i] < bound]
        pool, budget = sum([weights[i] for i in movable]), surplus
        for i in movable:
            extra = min(bound - counts[i], max(1, budget * weights[i] // pool), surplus)
            counts[i] = counts[i] + extra
            surplus = surplus - extra
    return np.array([bound] + counts)


def ragged_sizes(own_key, number_of, total, bound, skew):
    if number_of == 2:
        one = jax.random.randint(own_key, (), max(1, total - bound), min(bound, total - 1) + 1)
        return jnp.stack([one, total - one])
    tallies = jnp.asarray(profile(number_of, total, bound, skew), jnp.int32)
    twos = (number_of - 1) // 2
    donor, taker = tallies[1:1 + 2 * twos:2], tallies[2:2 + 2 * twos:2]
    margin = jnp.minimum(donor - 1, bound - taker)
    shifted = jax.random.randint(jax.random.fold_in(own_key, 1), (twos,), 0, 1 << 20) % (margin + 1)
    tallies = tallies.at[1:1 + 2 * twos:2].set(donor - shifted).at[2:2 + 2 * twos:2].set(taker + shifted)
    return tallies[jax.random.permutation(jax.random.fold_in(own_key, 2), number_of)]


def scatter_about(stream_key, shape, scale, bound, pieces=(), kind=jnp.bfloat16):
    gain = shard_levels(stream_key, shape, pieces, -0.22, 0.18) if pieces else 1.0
    entries = jax.random.normal(stream_key, shape, jnp.float32) * scale * gain
    return jnp.minimum(jnp.maximum(entries, -bound), bound).astype(kind)


def setup_inputs(seed: int = 0) -> dict:
    key_list = jax.random.split(jax.random.key(seed), 9)
    return {
        "query": draw_query(jax.random.fold_in(key_list[8], 71), 0),
        "resp_keys": scatter_about(key_list[1], (RESPONSES, RLEN, KVW), 1.0, 6.0, ((0, 32),)),
        "resp_values": scatter_about(key_list[2], (RESPONSES, RLEN, KVW), 1.0, 6.0, ((0, 32),)),
        "prompt_keys": draw_prompt_keys(jax.random.fold_in(key_list[8], 71), 0),
        "prompt_values": scatter_about(key_list[4], (PROMPTS, PLEN, KVW), 1.0, 6.0, ((1, 4),)),
        "out_grad": scatter_about(key_list[5], (RESPONSES, RLEN, QW), 1.0, 6.0, ((0, 32),)),
        "group": with_ends(jax.random.randint(key_list[6], (RESPONSES,), 0, PROMPTS), jax.random.fold_in(key_list[6], 1), 0, PROMPTS - 1).astype(jnp.int32),
        "lengths": ragged_sizes(key_list[7], RESPONSES, RESPONSES * RLEN * 5 // 8, RLEN, 2).astype(jnp.int32),
    }


masked_score = -1e+30

def one_response(query_rows, own_keys, own_values, grad_rows, length, front_keys, front_values):
    all_keys = jnp.concatenate([front_keys, own_keys], 0)
    all_values = jnp.concatenate([front_values, own_values], 0)
    total_len = all_keys.shape[0]
    score_scale = 1.0 / math.sqrt(HD)
    row_ids = jnp.arange(RLEN)[:, None]
    col_ids = jnp.arange(total_len)[None, :]
    allowed = (col_ids < PLEN) | (col_ids - PLEN <= row_ids)
    live_rows = (jnp.arange(RLEN) < length)[:, None]
    grad_rows = jnp.where(live_rows, grad_rows, jnp.zeros_like(grad_rows))
    group_size = QH // KVH
    query_four = query_rows.reshape(RLEN, KVH, group_size, HD).astype(jnp.float32)
    grad_four = grad_rows.reshape(RLEN, KVH, group_size, HD).astype(jnp.float32)
    query_parts = []
    key_parts = []
    value_parts = []
    for kv_head in range(KVH):
        head_keys = all_keys[:, kv_head * HD:(kv_head + 1) * HD].astype(jnp.float32)
        head_values = all_values[:, kv_head * HD:(kv_head + 1) * HD].astype(jnp.float32)
        head_query = query_four[:, kv_head]
        head_grad = grad_four[:, kv_head]
        scores = jnp.einsum('igd,jd->gij', head_query, head_keys) * score_scale
        scores = jnp.where(allowed[None], scores, masked_score)
        row_max = lax.optimization_barrier(jnp.max(scores, -1, keepdims=True))
        weights = jnp.where(allowed[None], jnp.exp(scores - row_max), 0.0)
        attn_prob = weights / lax.optimization_barrier(jnp.sum(weights, -1, keepdims=True))
        prob_low = lax.optimization_barrier(attn_prob.astype(jnp.bfloat16)).astype(jnp.float32)
        attn_out = jnp.einsum('gij,jd->igd', prob_low, head_values)
        delta = jnp.einsum('igd,igd->gi', head_grad, attn_out)
        dprob = jnp.einsum('igd,jd->gij', head_grad, head_values)
        dscore = attn_prob * (dprob - delta[:, :, None])
        dscore_low = lax.optimization_barrier(dscore.astype(jnp.bfloat16)).astype(jnp.float32)
        query_term = jnp.einsum('gij,jd->igd', dscore_low, head_keys) * score_scale
        key_term = jnp.einsum('gij,igd->jd', dscore_low, head_query) * score_scale
        value_term = jnp.einsum('gij,igd->jd', prob_low, head_grad)
        query_parts.append(query_term.reshape(RLEN, group_size * HD))
        key_parts.append(key_term)
        value_parts.append(value_term)
    query_grad = jnp.concatenate(query_parts, -1).astype(jnp.bfloat16)
    key_all = jnp.concatenate(key_parts, -1)
    value_all = jnp.concatenate(value_parts, -1)
    return (query_grad, key_all[PLEN:].astype(jnp.bfloat16), value_all[PLEN:].astype(jnp.bfloat16), key_all[:PLEN], value_all[:PLEN])

def reference(query, resp_keys, resp_values, prompt_keys, prompt_values, out_grad, group, lengths):

    def advance(totals, inputs_row):
        query_rows, own_keys, own_values, grad_rows, owner_id, length = inputs_row
        front_keys = lax.dynamic_index_in_dim(prompt_keys, owner_id, 0, keepdims=False)
        front_values = lax.dynamic_index_in_dim(prompt_values, owner_id, 0, keepdims=False)
        query_grad, key_grad, value_grad, prompt_key, prompt_value = one_response(query_rows, own_keys, own_values, grad_rows, length, front_keys, front_values)
        hit_mask = (jnp.arange(PROMPTS) == owner_id)[:, None, None]
        key_total = totals[0] + jnp.where(hit_mask, prompt_key[None], 0.0)
        value_total = totals[1] + jnp.where(hit_mask, prompt_value[None], 0.0)
        return ((key_total, value_total), (query_grad, key_grad, value_grad))
    zero_grads = jnp.zeros((PROMPTS, PLEN, KVW), jnp.float32)
    sums, stacked = lax.scan(advance, (zero_grads, zero_grads), (query, resp_keys, resp_values, out_grad, group, lengths))
    return (stacked[0], stacked[1], stacked[2], sums[0], sums[1])
```

```python
import functools
import math

import jax
import jax.numpy as jnp
from jax import lax
from jax.experimental import pallas as pl
from jax.experimental.pallas import tpu as pltpu
from jax.sharding import PartitionSpec as P

QH = 16
KVH = 4
HD = 128
GROUP = QH // KVH
TILE = 128
MESH = pl.DeviceIdType.MESH
MASKED = -1e30
SCALE = 1.0 / math.sqrt(HD)
NT = (((1,), (1,)), ((), ()))
NN = (((1,), (0,)), ((), ()))
TN = (((0,), (0,)), ((), ()))


def dot(a, b, dims):
    return lax.dot_general(a, b, dims, preferred_element_type=jnp.float32)


def kernel(
    n_p, n_r, order,
    group_ref, length_ref, query_hbm, grad_hbm, rkeys_hbm, rvalues_hbm, pkeys_ref, pvalues_ref,
    dquery_hbm, dkey_hbm, dvalue_hbm, dpkey_ref, dpvalue_ref,
    query_v, grad_v, keys_v, values_v, dscore_v, dquery_v, dkey_v, dvalue_v,
    front_send, front_recv, part_send, part_recv, total_v,
    load_sem, store_sem, front_ssem, front_rsem, part_ssem, part_rsem, total_ssem, total_rsem,
):
    rows = query_v.shape[0]
    own = pkeys_ref.shape[1]
    front = own * n_p
    prompts = pkeys_ref.shape[0]
    tiles = rows // TILE
    wide = GROUP * HD
    n_dev = n_p * n_r
    me_p = lax.axis_index("prompt")
    me_r = lax.axis_index("resp")
    me = me_p * n_r + me_r
    stride = n_r // KVH

    loads = {}
    loads["k"] = pltpu.make_async_copy(
        rkeys_hbm.at[0], keys_v.at[pl.ds(front, rows)], load_sem.at[0])
    loads["v"] = pltpu.make_async_copy(
        rvalues_hbm.at[0], values_v.at[pl.ds(front, rows)], load_sem.at[1])
    loads["k"].start()
    loads["v"].start()
    for i, h in enumerate(order):
        cols = pl.ds(h * wide, wide)
        loads["q", h] = pltpu.make_async_copy(
            query_hbm.at[0, :, cols], query_v.at[:, cols], load_sem.at[2 + 2 * i])
        loads["g", h] = pltpu.make_async_copy(
            grad_hbm.at[0, :, cols], grad_v.at[:, cols], load_sem.at[3 + 2 * i])
        loads["q", h].start()
        loads["g", h].start()

    barrier = pltpu.get_barrier_semaphore()

    @pl.loop(1, n_dev)
    def _(step):
        peer = lax.rem(me + step, n_dev)
        pl.semaphore_signal(
            barrier, inc=1, device_id=(peer // n_r, lax.rem(peer, n_r)), device_id_type=MESH)

    def front_of(q):
        prompt = group_ref[q * n_r + me_r]
        return jnp.concatenate(
            [pkeys_ref[prompt].astype(jnp.float32), pvalues_ref[prompt].astype(jnp.float32)], 0
        ).astype(jnp.bfloat16)

    for q in range(n_p):
        front_send[q] = front_of(q)
    front_recv[me_p] = front_of(me_p)
    pl.semaphore_wait(barrier, n_dev - 1)

    front_copies = []
    for step in range(1, n_p):
        to = lax.rem(me_p + step, n_p)
        copy = pltpu.make_async_remote_copy(
            src_ref=front_send.at[to], dst_ref=front_recv.at[me_p],
            send_sem=front_ssem.at[step], recv_sem=front_rsem.at[me_p],
            device_id=(to, me_r), device_id_type=MESH)
        copy.start()
        front_copies.append(copy)

    live = jnp.where(
        lax.broadcasted_iota(jnp.int32, (rows, HD), 0) < length_ref[0], 1.0, 0.0
    ).astype(jnp.bfloat16)
    allowed = (
        lax.broadcasted_iota(jnp.int32, (TILE, GROUP * TILE), 0)
        <= lax.broadcasted_iota(jnp.int32, (TILE, GROUP * TILE), 1) % TILE
    )

    for step in range(1, n_p):
        source = lax.rem(me_p + step, n_p)
        pltpu.make_async_remote_copy(
            src_ref=front_send.at[source], dst_ref=front_recv.at[source],
            send_sem=front_ssem.at[step], recv_sem=front_rsem.at[source],
            device_id=(source, me_r), device_id_type=MESH).wait_recv()
    loads["k"].wait()
    loads["v"].wait()
    arrived = [front_recv[q].astype(jnp.float32) for q in range(n_p)]
    keys_v[0:front] = jnp.concatenate([a[0:own] for a in arrived], 0).astype(jnp.bfloat16)
    values_v[0:front] = jnp.concatenate([a[own:] for a in arrived], 0).astype(jnp.bfloat16)

    def stacked(ref, h, t):
        return jnp.concatenate(
            [ref[t * TILE:(t + 1) * TILE, (h * GROUP + g) * HD:(h * GROUP + g + 1) * HD]
             for g in range(GROUP)], 0)

    def part_copy(i, step):
        to = lax.rem(me_p + step, n_p)
        return pltpu.make_async_remote_copy(
            src_ref=part_send.at[i, to], dst_ref=part_recv.at[me],
            send_sem=part_ssem.at[i, step], recv_sem=part_rsem,
            device_id=(to, order[i] * stride), device_id_type=MESH)

    def first_pass(i):
        h = order[i]
        loads["q", h].wait()
        loads["g", h].wait()
        lanes = slice(h * HD, (h + 1) * HD)
        key_sums, value_sums = [], []
        for t in range(tiles):
            depth = front + (t + 1) * TILE
            query = stacked(query_v, h, t)
            grad = stacked(grad_v, h, t) * jnp.concatenate(
                [live[t * TILE:(t + 1) * TILE]] * GROUP, 0)
            scores = dot(keys_v[0:depth, lanes], query, NT)
            scores = jnp.concatenate(
                [scores[:depth - TILE], jnp.where(allowed, scores[depth - TILE:], MASKED)], 0)
            top = jnp.max(scores, 0, keepdims=True)
            weights = jnp.exp2((scores - top) * (SCALE * math.log2(math.e)))
            prob = weights * (1.0 / jnp.sum(weights, 0, keepdims=True))
            dprob = dot(values_v[0:depth, lanes], grad, NT)
            delta = jnp.sum(prob * dprob, 0, keepdims=True)
            dscore = (prob * (dprob - delta)).astype(jnp.bfloat16)
            dscore_v[h, t, 0:depth] = dscore
            value_sums.append(dot(prob.astype(jnp.bfloat16), grad, NN))
            key_sums.append(dot(dscore, query, NN))
        front_key = sum(s[:front] for s in key_sums) * SCALE
        front_value = sum(s[:front] for s in value_sums)
        for q in range(n_p):
            part_send[i, q] = jnp.concatenate(
                [front_key[q * own:(q + 1) * own], front_value[q * own:(q + 1) * own]], 0
            ).astype(jnp.bfloat16)

        @pl.when(me_r != h * stride)
        def _():
            part_copy(i, 0).start()

        @pl.when(me_r == h * stride)
        def _():
            part_recv[me] = part_send[i, me_p]

        for step in range(1, n_p):
            part_copy(i, step).start()
        for t in range(tiles):
            low = front + t * TILE
            span = slice(t * TILE, (t + 1) * TILE)
            dkey_v[span, lanes] = (
                sum(s[low:low + TILE] for s in key_sums[t:]) * SCALE).astype(jnp.bfloat16)
            dvalue_v[span, lanes] = sum(
                s[low:low + TILE] for s in value_sums[t:]).astype(jnp.bfloat16)

    def total_copy(i, step):
        return pltpu.make_async_remote_copy(
            src_ref=total_v.at[i], dst_ref=total_v.at[i],
            send_sem=total_ssem.at[step], recv_sem=total_rsem.at[i],
            device_id=(me_p, lax.rem(me_r + step, n_r)), device_id_type=MESH)

    def add_up(i):
        @pl.when(me_r == order[i] * stride)
        def _():
            others = part_recv.at[pl.ds(0, n_dev - 1)]
            pltpu.make_async_copy(others, others, part_rsem).wait()

            def body(s, totals):
                prompt = group_ref[s]
                piece = part_recv[s].astype(jnp.float32)
                return tuple(
                    total + jnp.where(prompt == p, piece, 0.0) for p, total in enumerate(totals))

            zero = jnp.zeros(part_recv.shape[1:], jnp.float32)
            totals = lax.fori_loop(0, n_dev, body, (zero,) * prompts)
            for p in range(prompts):
                total_v[i, p] = totals[p].astype(jnp.bfloat16)
            for step in range(1, n_r):
                total_copy(i, step).start()

    stores = []

    def second_pass(i):
        h = order[i]
        lanes = slice(h * HD, (h + 1) * HD)
        for t in range(tiles):
            depth = front + (t + 1) * TILE
            turned = dot(keys_v[0:depth, lanes], dscore_v[h, t, 0:depth], TN) * SCALE
            for g in range(GROUP):
                dquery_v[t * TILE:(t + 1) * TILE, (h * GROUP + g) * HD:(h * GROUP + g + 1) * HD] = (
                    turned[:, g * TILE:(g + 1) * TILE].T.astype(jnp.bfloat16))
        cols = pl.ds(h * wide, wide)
        copy = pltpu.make_async_copy(
            dquery_v.at[:, cols], dquery_hbm.at[0, :, cols], store_sem.at[2 + i])
        copy.start()
        stores.append(copy)

    first_pass(0)
    first_pass(1)
    first_pass(2)
    add_up(0)
    first_pass(3)
    for n, (ref, out) in enumerate(((dkey_v, dkey_hbm), (dvalue_v, dvalue_hbm))):
        copy = pltpu.make_async_copy(ref, out.at[0], store_sem.at[n])
        copy.start()
        stores.append(copy)
    add_up(1)
    second_pass(0)
    second_pass(1)
    add_up(2)
    second_pass(2)
    second_pass(3)
    add_up(3)

    for i, h in enumerate(order):
        @pl.when(me_r != h * stride)
        def _():
            total_copy(i, 1).wait_recv()

        dpkey_ref[:, :, h * HD:(h + 1) * HD] = total_v[i].astype(jnp.float32)[:, 0:own]
        dpvalue_ref[:, :, h * HD:(h + 1) * HD] = total_v[i].astype(jnp.float32)[:, own:]

    for copy in stores:
        copy.wait()
    for copy in front_copies:
        copy.wait_send()
    for i, h in enumerate(order):
        @pl.when(me_r != h * stride)
        def _():
            part_copy(i, 0).wait_send()

        for step in range(1, n_p):
            part_copy(i, step).wait_send()

        @pl.when(me_r == h * stride)
        def _():
            for step in range(1, n_r):
                total_copy(i, step).wait_send()


def shards(n_p, n_r, query, resp_keys, resp_values, prompt_keys, prompt_values, out_grad, group, lengths):
    rows = query.shape[1]
    prompts, own, kvw = prompt_keys.shape
    front = own * n_p
    n_dev = n_p * n_r
    order = (0, 3, 1, 2)
    low = jnp.bfloat16
    vmem = pl.BlockSpec(memory_space=pltpu.VMEM)
    smem = pl.BlockSpec(memory_space=pltpu.SMEM)
    hbm = pl.BlockSpec(memory_space=pl.ANY)
    dma = pltpu.SemaphoreType.DMA
    return pl.pallas_call(
        functools.partial(kernel, n_p, n_r, order),
        out_shape=(
            jax.ShapeDtypeStruct(query.shape, low),
            jax.ShapeDtypeStruct(resp_keys.shape, low),
            jax.ShapeDtypeStruct(resp_values.shape, low),
            jax.ShapeDtypeStruct(prompt_keys.shape, jnp.float32),
            jax.ShapeDtypeStruct(prompt_values.shape, jnp.float32),
        ),
        in_specs=[smem, smem, hbm, hbm, hbm, hbm, vmem, vmem],
        out_specs=(hbm, hbm, hbm, vmem, vmem),
        scratch_shapes=[
            pltpu.VMEM((rows, QH * HD), low),
            pltpu.VMEM((rows, QH * HD), low),
            pltpu.VMEM((front + rows, kvw), low),
            pltpu.VMEM((front + rows, kvw), low),
            pltpu.VMEM((KVH, rows // TILE, front + rows, GROUP * TILE), low),
            pltpu.VMEM((rows, QH * HD), low),
            pltpu.VMEM((rows, kvw), low),
            pltpu.VMEM((rows, kvw), low),
            pltpu.VMEM((n_p, 2 * own, kvw), low),
            pltpu.VMEM((n_p, 2 * own, kvw), low),
            pltpu.VMEM((KVH, n_p, 2 * own, HD), low),
            pltpu.VMEM((n_dev, 2 * own, HD), low),
            pltpu.VMEM((KVH, prompts, 2 * own, HD), low),
            dma((2 + 2 * KVH,)),
            dma((2 + KVH,)),
            dma((n_p,)),
            dma((n_p,)),
            dma((KVH, n_p)),
            dma,
            dma((n_r,)),
            dma((KVH,)),
        ],
        compiler_params=pltpu.CompilerParams(
            collective_id=0, has_side_effects=True, vmem_limit_bytes=50 * 1024 * 1024),
    )(group, lengths, query, out_grad, resp_keys, resp_values, prompt_keys, prompt_values)


def solution(mesh):
    return jax.shard_map(
        functools.partial(shards, mesh.shape["prompt"], mesh.shape["resp"]),
        mesh=mesh,
        in_specs=(
            P(("prompt", "resp"), None, None),
            P(("prompt", "resp"), None, None),
            P(("prompt", "resp"), None, None),
            P(None, "prompt", None),
            P(None, "prompt", None),
            P(("prompt", "resp"), None, None),
            P(),
            P(("prompt", "resp")),
        ),
        out_specs=(
            P(("prompt", "resp"), None, None),
            P(("prompt", "resp"), None, None),
            P(("prompt", "resp"), None, None),
            P(None, "prompt", None),
            P(None, "prompt", None),
        ),
        check_vma=False,
    )
```

```python
import functools
import math

import jax
import jax.numpy as jnp
from jax import lax
from jax.experimental import pallas as pl
from jax.experimental.pallas import tpu as pltpu
from jax.sharding import PartitionSpec as P

QH = 16
KVH = 4
HD = 128
GROUP = QH // KVH
TILE = 128
MESH = pl.DeviceIdType.MESH
MASKED = -1e30
SCALE = 1.0 / math.sqrt(HD)
NT = (((1,), (1,)), ((), ()))
NN = (((1,), (0,)), ((), ()))
TN = (((0,), (0,)), ((), ()))


def dot(a, b, dims):
    return lax.dot_general(a, b, dims, preferred_element_type=jnp.float32)


def kernel(
    n_p, n_r, order,
    group_ref, length_ref, query_hbm, grad_hbm, rkeys_hbm, rvalues_hbm, pkeys_hbm, pvalues_hbm,
    dquery_hbm, dkey_hbm, dvalue_hbm, total_ref,
    query_v, grad_v, live_grad_v, keys_v, values_v, pkeys_v, pvalues_v,
    weight_v, dprob_v, stat_v, dfront_v, dquery_v, dkey_v, dvalue_v,
    front_send, front_recv, part_send, part_recv, total_v,
    load_sem, store_sem, front_ssem, front_rsem, part_ssem, part_rsem, total_ssem, total_rsem,
):
    rows = query_v.shape[0]
    prompts, own = pkeys_v.shape[:2]
    front = own * n_p
    tiles = rows // TILE
    wide = GROUP * HD
    n_dev = n_p * n_r
    me_p = lax.axis_index("prompt")
    me_r = lax.axis_index("resp")
    me = me_p * n_r + me_r
    stride = n_r // KVH
    power = SCALE * math.log2(math.e)

    barrier = pltpu.get_barrier_semaphore()

    @pl.loop(1, n_dev)
    def _(step):
        peer = lax.rem(me + step, n_dev)
        pl.semaphore_signal(
            barrier, inc=1, device_id=(peer // n_r, lax.rem(peer, n_r)), device_id_type=MESH)

    loads = {}
    resp = pl.ds(front, rows)
    wanted = [("k", rkeys_hbm.at[0], keys_v.at[resp])]
    for h in order:
        cols = pl.ds(h * wide, wide)
        wanted.append((("q", h), query_hbm.at[0, :, cols], query_v.at[:, cols]))
        wanted.append((("g", h), grad_hbm.at[0, :, cols], grad_v.at[:, cols]))
        if h == order[0]:
            wanted.append(("v", rvalues_hbm.at[0], values_v.at[resp]))
            wanted.append(("pk", pkeys_hbm, pkeys_v))
            wanted.append(("pv", pvalues_hbm, pvalues_v))
    for n, (name, src, dst) in enumerate(wanted):
        loads[name] = pltpu.make_async_copy(src, dst, load_sem.at[n])
        loads[name].start()

    live = jnp.where(
        lax.broadcasted_iota(jnp.int32, (rows, HD), 0) < length_ref[0], 1.0, 0.0
    ).astype(jnp.bfloat16)
    allowed = (
        lax.broadcasted_iota(jnp.int32, (TILE, GROUP * TILE), 0)
        <= lax.broadcasted_iota(jnp.int32, (TILE, GROUP * TILE), 1) % TILE
    )

    def stacked(ref, h, t):
        return jnp.concatenate(
            [ref[t * TILE:(t + 1) * TILE, (h * GROUP + g) * HD:(h * GROUP + g + 1) * HD]
             for g in range(GROUP)], 0)

    def lanes_of(h):
        return slice(h * HD, (h + 1) * HD)

    def resp_scores(i):
        h = order[i]
        lanes = lanes_of(h)
        loads["q", h].wait()
        loads["g", h].wait()
        for t in range(tiles):
            depth = (t + 1) * TILE
            query = stacked(query_v, h, t)
            grad = stacked(grad_v, h, t) * jnp.concatenate(
                [live[t * TILE:(t + 1) * TILE]] * GROUP, 0)
            live_grad_v[h, t] = grad
            scores = dot(keys_v[front:front + depth, lanes], query, NT)
            last = jnp.where(allowed, scores[depth - TILE:], MASKED)
            scores = jnp.concatenate([scores[:depth - TILE], last], 0) if t else last
            top = jnp.max(scores, 0, keepdims=True)
            weights = jnp.exp2((scores - top) * power)
            dprob = dot(values_v[front:front + depth, lanes], grad, NT)
            weight_v[h, t, 0:depth] = weights
            dprob_v[h, t, 0:depth] = dprob
            stat_v[h, t, 0:1] = top
            stat_v[h, t, 1:2] = jnp.sum(weights, 0, keepdims=True)
            stat_v[h, t, 2:3] = jnp.sum(weights * dprob, 0, keepdims=True)

    def part_copy(i, step):
        to = lax.rem(me_p + step, n_p)
        return pltpu.make_async_remote_copy(
            src_ref=part_send.at[i, to], dst_ref=part_recv.at[me],
            send_sem=part_ssem.at[i, step], recv_sem=part_rsem,
            device_id=(to, order[i] * stride), device_id_type=MESH)

    def front_terms(i):
        h = order[i]
        lanes = lanes_of(h)
        front_key, front_value = 0.0, 0.0
        for t in range(tiles):
            query = stacked(query_v, h, t)
            grad = live_grad_v[h, t]
            resp_top = stat_v[h, t, 0:1]
            scores = dot(keys_v[0:front, lanes], query, NT)
            dprob = dot(values_v[0:front, lanes], grad, NT)
            top = jnp.maximum(resp_top, jnp.max(scores, 0, keepdims=True))
            shrink = jnp.exp2((resp_top - top) * power)
            weights = jnp.exp2((scores - top) * power)
            inverse = 1.0 / (shrink * stat_v[h, t, 1:2] + jnp.sum(weights, 0, keepdims=True))
            factor = shrink * inverse
            prob = weights * inverse
            delta = factor * stat_v[h, t, 2:3] + jnp.sum(prob * dprob, 0, keepdims=True)
            dscore = (prob * (dprob - delta)).astype(jnp.bfloat16)
            dfront_v[h, t] = dscore
            stat_v[h, t, 3:4] = factor
            stat_v[h, t, 4:5] = delta
            front_value += dot(prob.astype(jnp.bfloat16), grad, NN)
            front_key += dot(dscore, query, NN)
        front_key = front_key * SCALE
        for q in range(n_p):
            part_send[i, q] = jnp.concatenate(
                [front_key[q * own:(q + 1) * own], front_value[q * own:(q + 1) * own]], 0
            ).astype(jnp.bfloat16)

        @pl.when(me_r != h * stride)
        def _():
            part_copy(i, 0).start()

        @pl.when(me_r == h * stride)
        def _():
            part_recv[me] = part_send[i, me_p]

        for step in range(1, n_p):
            part_copy(i, step).start()

    def total_copy(i, step):
        return pltpu.make_async_remote_copy(
            src_ref=total_v.at[i], dst_ref=total_v.at[i],
            send_sem=total_ssem.at[step], recv_sem=total_rsem.at[i],
            device_id=(me_p, lax.rem(me_r + step, n_r)), device_id_type=MESH)

    def add_up(i):
        @pl.when(me_r == order[i] * stride)
        def _():
            others = part_recv.at[pl.ds(0, n_dev - 1)]
            pltpu.make_async_copy(others, others, part_rsem).wait()

            def body(s, totals):
                prompt = group_ref[s]
                piece = part_recv[s].astype(jnp.float32)
                return tuple(
                    total + jnp.where(prompt == p, piece, 0.0) for p, total in enumerate(totals))

            zero = jnp.zeros(part_recv.shape[1:], jnp.float32)
            totals = lax.fori_loop(0, n_dev, body, (zero,) * prompts)
            for p in range(prompts):
                total_v[i, p] = totals[p].astype(jnp.bfloat16)
            for step in range(1, n_r):
                total_copy(i, step).start()

    stores = []

    def store(ref, out):
        copy = pltpu.make_async_copy(ref, out, store_sem.at[len(stores)])
        copy.start()
        stores.append(copy)

    def resp_terms(i):
        h = order[i]
        lanes = lanes_of(h)
        key_sums, value_sums = [], []
        for t in range(tiles):
            depth = (t + 1) * TILE
            query = stacked(query_v, h, t)
            prob = weight_v[h, t, 0:depth] * stat_v[h, t, 3:4]
            dscore = (prob * (dprob_v[h, t, 0:depth] - stat_v[h, t, 4:5])).astype(jnp.bfloat16)
            value_sums.append(dot(prob.astype(jnp.bfloat16), live_grad_v[h, t], NN))
            key_sums.append(dot(dscore, query, NN))
            turned = dot(
                keys_v[0:front + depth, lanes],
                jnp.concatenate([dfront_v[h, t], dscore], 0), TN) * SCALE
            for g in range(GROUP):
                dquery_v[t * TILE:(t + 1) * TILE, (h * GROUP + g) * HD:(h * GROUP + g + 1) * HD] = (
                    turned[:, g * TILE:(g + 1) * TILE].T.astype(jnp.bfloat16))
        for t in range(tiles):
            span = slice(t * TILE, (t + 1) * TILE)
            dkey_v[span, lanes] = (
                sum(s[span] for s in key_sums[t:]) * SCALE).astype(jnp.bfloat16)
            dvalue_v[span, lanes] = sum(s[span] for s in value_sums[t:]).astype(jnp.bfloat16)
        cols = pl.ds(h * wide, wide)
        store(dquery_v.at[:, cols], dquery_hbm.at[0, :, cols])

    loads["k"].wait()
    loads["v"].wait()
    resp_scores(0)

    loads["pk"].wait()
    loads["pv"].wait()

    def front_of(q):
        prompt = group_ref[q * n_r + me_r]
        return jnp.concatenate(
            [pkeys_v[prompt].astype(jnp.float32), pvalues_v[prompt].astype(jnp.float32)], 0
        ).astype(jnp.bfloat16)

    for q in range(n_p):
        front_send[q] = front_of(q)
    front_recv[me_p] = front_of(me_p)
    pl.semaphore_wait(barrier, n_dev - 1)

    front_copies = []
    for step in range(1, n_p):
        to = lax.rem(me_p + step, n_p)
        copy = pltpu.make_async_remote_copy(
            src_ref=front_send.at[to], dst_ref=front_recv.at[me_p],
            send_sem=front_ssem.at[step], recv_sem=front_rsem.at[me_p],
            device_id=(to, me_r), device_id_type=MESH)
        copy.start()
        front_copies.append(copy)

    for i in range(1, KVH):
        resp_scores(i)

    for step in range(1, n_p):
        source = lax.rem(me_p + step, n_p)
        pltpu.make_async_remote_copy(
            src_ref=front_send.at[source], dst_ref=front_recv.at[source],
            send_sem=front_ssem.at[step], recv_sem=front_rsem.at[source],
            device_id=(source, me_r), device_id_type=MESH).wait_recv()
    arrived = [front_recv[q].astype(jnp.float32) for q in range(n_p)]
    keys_v[0:front] = jnp.concatenate([a[0:own] for a in arrived], 0).astype(jnp.bfloat16)
    values_v[0:front] = jnp.concatenate([a[own:] for a in arrived], 0).astype(jnp.bfloat16)

    for i in range(KVH):
        front_terms(i)
    resp_terms(0)
    resp_terms(1)
    for i in range(KVH):
        add_up(i)
    resp_terms(2)
    resp_terms(3)
    store(dkey_v, dkey_hbm.at[0])
    store(dvalue_v, dvalue_hbm.at[0])

    for i, h in enumerate(order):
        @pl.when(me_r != h * stride)
        def _():
            total_copy(i, 1).wait_recv()

        total_ref[h] = total_v[i]

    for copy in stores:
        copy.wait()
    for copy in front_copies:
        copy.wait_send()
    for i, h in enumerate(order):
        @pl.when(me_r != h * stride)
        def _():
            part_copy(i, 0).wait_send()

        for step in range(1, n_p):
            part_copy(i, step).wait_send()

        @pl.when(me_r == h * stride)
        def _():
            for step in range(1, n_r):
                total_copy(i, step).wait_send()


def write_out(dquery, dkey, dvalue, total, dquery_out, dkey_out, dvalue_out, dpkey, dpvalue, sem):
    copies = []
    for n, (src, dst) in enumerate(
            ((dquery, dquery_out), (dkey, dkey_out), (dvalue, dvalue_out))):
        copies.append(pltpu.make_async_copy(src, dst, sem.at[n]))
        copies[-1].start()
    own = dpkey.shape[1]
    for h in range(KVH):
        both = total[h].astype(jnp.float32)
        dpkey[:, :, h * HD:(h + 1) * HD] = both[:, 0:own]
        dpvalue[:, :, h * HD:(h + 1) * HD] = both[:, own:]
    for copy in copies:
        copy.wait()


def shards(n_p, n_r, query, resp_keys, resp_values, prompt_keys, prompt_values, out_grad, group, lengths):
    rows = query.shape[1]
    prompts, own, kvw = prompt_keys.shape
    front = own * n_p
    n_dev = n_p * n_r
    tiles = rows // TILE
    order = (0, 3, 1, 2)
    low = jnp.bfloat16
    vmem = pl.BlockSpec(memory_space=pltpu.VMEM)
    smem = pl.BlockSpec(memory_space=pltpu.SMEM)
    some = pl.BlockSpec(memory_space=pl.ANY)
    hbm = pl.BlockSpec(memory_space=pltpu.HBM)
    dma = pltpu.SemaphoreType.DMA
    like = lambda x, dtype: jax.ShapeDtypeStruct(x.shape, dtype)
    dquery, dkey, dvalue, total = pl.pallas_call(
        functools.partial(kernel, n_p, n_r, order),
        out_shape=(
            like(query, low), like(resp_keys, low), like(resp_values, low),
            jax.ShapeDtypeStruct((KVH, prompts, 2 * own, HD), low),
        ),
        in_specs=[smem, smem] + [hbm] * 6,
        out_specs=(some, some, some, vmem),
        scratch_shapes=[
            pltpu.VMEM((rows, QH * HD), low),
            pltpu.VMEM((rows, QH * HD), low),
            pltpu.VMEM((KVH, tiles, GROUP * TILE, HD), low),
            pltpu.VMEM((front + rows, kvw), low),
            pltpu.VMEM((front + rows, kvw), low),
            pltpu.VMEM((prompts, own, kvw), low),
            pltpu.VMEM((prompts, own, kvw), low),
            pltpu.VMEM((KVH, tiles, rows, GROUP * TILE), jnp.float32),
            pltpu.VMEM((KVH, tiles, rows, GROUP * TILE), jnp.float32),
            pltpu.VMEM((KVH, tiles, 8, GROUP * TILE), jnp.float32),
            pltpu.VMEM((KVH, tiles, front, GROUP * TILE), low),
            pltpu.VMEM((rows, QH * HD), low),
            pltpu.VMEM((rows, kvw), low),
            pltpu.VMEM((rows, kvw), low),
            pltpu.VMEM((n_p, 2 * own, kvw), low),
            pltpu.VMEM((n_p, 2 * own, kvw), low),
            pltpu.VMEM((KVH, n_p, 2 * own, HD), low),
            pltpu.VMEM((n_dev, 2 * own, HD), low),
            pltpu.VMEM((KVH, prompts, 2 * own, HD), low),
            dma((5 + 2 * KVH,)),
            dma((2 + KVH,)),
            dma((n_p,)),
            dma((n_p,)),
            dma((KVH, n_p)),
            dma,
            dma((n_r,)),
            dma((KVH,)),
        ],
        compiler_params=pltpu.CompilerParams(
            collective_id=0, has_side_effects=True, vmem_limit_bytes=60 * 1024 * 1024),
    )(group, lengths, query, out_grad, resp_keys, resp_values, prompt_keys, prompt_values)
    return pl.pallas_call(
        write_out,
        out_shape=(
            like(query, low), like(resp_keys, low), like(resp_values, low),
            like(prompt_keys, jnp.float32), like(prompt_values, jnp.float32),
        ),
        in_specs=[some, some, some, vmem],
        out_specs=(some, some, some, vmem, vmem),
        scratch_shapes=[dma((3,))],
        compiler_params=pltpu.CompilerParams(vmem_limit_bytes=60 * 1024 * 1024),
    )(dquery, dkey, dvalue, total)


def solution(mesh):
    return jax.shard_map(
        functools.partial(shards, mesh.shape["prompt"], mesh.shape["resp"]),
        mesh=mesh,
        in_specs=(
            P(("prompt", "resp"), None, None),
            P(("prompt", "resp"), None, None),
            P(("prompt", "resp"), None, None),
            P(None, "prompt", None),
            P(None, "prompt", None),
            P(("prompt", "resp"), None, None),
            P(),
            P(("prompt", "resp")),
        ),
        out_specs=(
            P(("prompt", "resp"), None, None),
            P(("prompt", "resp"), None, None),
            P(("prompt", "resp"), None, None),
            P(None, "prompt", None),
            P(None, "prompt", None),
        ),
        check_vma=False,
    )
```

```python
import functools
import math

import jax
import jax.numpy as jnp
from jax import lax
from jax.experimental import pallas as pl
from jax.experimental.pallas import tpu as pltpu
from jax.sharding import PartitionSpec as P

QH = 16
KVH = 4
HD = 128
GROUP = QH // KVH
TILE = 128
PIECES = 4
MESH = pl.DeviceIdType.MESH
MASKED = -1e30
SCALE = 1.0 / math.sqrt(HD)
NT = (((1,), (1,)), ((), ()))
NN = (((1,), (0,)), ((), ()))
TN = (((0,), (0,)), ((), ()))


def dot(a, b, dims):
    return lax.dot_general(a, b, dims, preferred_element_type=jnp.float32)


def kernel(
    n_p, n_r, order,
    group_ref, length_ref, query_hbm, grad_hbm, rkeys_hbm, rvalues_hbm, pkeys_hbm, pvalues_hbm,
    dquery_hbm, dkey_hbm, dvalue_hbm, total_ref,
    query_v, grad_v, live_grad_v, keys_v, values_v, pkeys_v, pvalues_v,
    bias_v, weight_v, dprob_v, stat_v, dfront_v, dquery_v, dkey_v, dvalue_v,
    front_send, front_recv, part_send, part_recv, total_v,
    load_sem, store_sem, front_ssem, front_rsem, part_ssem, part_rsem, total_ssem, total_rsem,
):
    rows = query_v.shape[0]
    prompts, own = pkeys_v.shape[:2]
    front = own * n_p
    tiles = rows // TILE
    wide = GROUP * HD
    n_dev = n_p * n_r
    me_p = lax.axis_index("prompt")
    me_r = lax.axis_index("resp")
    me = me_p * n_r + me_r
    stride = n_r // KVH
    power = SCALE * math.log2(math.e)

    barrier = pltpu.get_barrier_semaphore()

    def ahead(place, step, size):
        later = place + step
        return jnp.where(later >= size, later - size, later)

    peers_p = [ahead(me_p, step, n_p) for step in range(n_p)]
    peers_r = [ahead(me_r, step, n_r) for step in range(n_r)]
    for to_p in peers_p:
        for to_r in peers_r:
            if to_p is not peers_p[0] or to_r is not peers_r[0]:
                pl.semaphore_signal(
                    barrier, inc=1, device_id=(to_p, to_r), device_id_type=MESH)

    loads = {}
    resp = pl.ds(front, rows)
    wanted = [("k", rkeys_hbm.at[0], keys_v.at[resp])]
    for h in order:
        cols = pl.ds(h * wide, wide)
        wanted.append((("q", h), query_hbm.at[0, :, cols], query_v.at[:, cols]))
        wanted.append((("g", h), grad_hbm.at[0, :, cols], grad_v.at[:, cols]))
        if h == order[0]:
            wanted.append(("v", rvalues_hbm.at[0], values_v.at[resp]))
            wanted.append(("pk", pkeys_hbm, pkeys_v))
            wanted.append(("pv", pvalues_hbm, pvalues_v))
    for n, (name, src, dst) in enumerate(wanted):
        loads[name] = pltpu.make_async_copy(src, dst, load_sem.at[n])
        loads[name].start()

    live = jnp.where(
        lax.broadcasted_iota(jnp.int32, (rows, HD), 0) < length_ref[0], 1.0, 0.0
    ).astype(jnp.bfloat16)
    bias_v[...] = jnp.where(
        lax.broadcasted_iota(jnp.int32, (TILE, TILE), 0)
        <= lax.broadcasted_iota(jnp.int32, (TILE, TILE), 1), 0.0, MASKED)

    def stacked(ref, h, t, start=0, stop=GROUP):
        return jnp.concatenate(
            [ref[t * TILE:(t + 1) * TILE, (h * GROUP + g) * HD:(h * GROUP + g + 1) * HD]
             for g in range(start, stop)], 0)

    def lanes_of(h):
        return slice(h * HD, (h + 1) * HD)

    def resp_scores(i):
        h = order[i]
        lanes = lanes_of(h)
        loads["q", h].wait()
        loads["g", h].wait()
        for t in range(tiles):
            depth = (t + 1) * TILE
            for g in range(0, GROUP, 2):
                query = stacked(query_v, h, t, g, g + 2)
                grad = stacked(grad_v, h, t, g, g + 2) * jnp.concatenate(
                    [live[t * TILE:(t + 1) * TILE]] * 2, 0)
                span = slice(g * TILE, (g + 2) * TILE)
                live_grad_v[h, t, span] = grad
                scores = dot(keys_v[front:front + depth, lanes], query, NT)
                last = scores[depth - TILE:] + jnp.concatenate([bias_v[...]] * 2, 1)
                scores = jnp.concatenate([scores[:depth - TILE], last], 0) if t else last
                top = jnp.max(scores, 0, keepdims=True)
                weights = jnp.exp2((scores - top) * power)
                dprob = dot(values_v[front:front + depth, lanes], grad, NT)
                weight_v[h, t, 0:depth, span] = weights
                dprob_v[h, t, 0:depth, span] = dprob
                stat_v[h, t, 0:1, span] = top
                stat_v[h, t, 1:2, span] = jnp.sum(weights, 0, keepdims=True)
                stat_v[h, t, 2:3, span] = jnp.sum(weights * dprob, 0, keepdims=True)

    def part_copy(i, step):
        to = peers_p[step]
        return pltpu.make_async_remote_copy(
            src_ref=part_send.at[i, to], dst_ref=part_recv.at[me],
            send_sem=part_ssem.at[i, step], recv_sem=part_rsem,
            device_id=(to, order[i] * stride), device_id_type=MESH)

    def front_terms(i):
        h = order[i]
        lanes = lanes_of(h)
        front_key, front_value = 0.0, 0.0
        for t in range(tiles):
            query = stacked(query_v, h, t)
            grad = live_grad_v[h, t]
            resp_top = stat_v[h, t, 0:1]
            scores = dot(keys_v[0:front, lanes], query, NT)
            dprob = dot(values_v[0:front, lanes], grad, NT)
            top = jnp.maximum(resp_top, jnp.max(scores, 0, keepdims=True))
            shrink = jnp.exp2((resp_top - top) * power)
            weights = jnp.exp2((scores - top) * power)
            inverse = 1.0 / (shrink * stat_v[h, t, 1:2] + jnp.sum(weights, 0, keepdims=True))
            factor = shrink * inverse
            prob = weights * inverse
            delta = factor * stat_v[h, t, 2:3] + jnp.sum(prob * dprob, 0, keepdims=True)
            dscore = (prob * (dprob - delta)).astype(jnp.bfloat16)
            dfront_v[h, t] = dscore
            stat_v[h, t, 3:4] = factor
            stat_v[h, t, 4:5] = delta
            front_value += dot(prob.astype(jnp.bfloat16), grad, NN)
            front_key += dot(dscore, query, NN)
        front_key = front_key * SCALE
        for q in range(n_p):
            part_send[i, q] = jnp.concatenate(
                [front_key[q * own:(q + 1) * own], front_value[q * own:(q + 1) * own]], 0
            ).astype(jnp.bfloat16)

        @pl.when(me_r != h * stride)
        def _():
            part_copy(i, 0).start()

        @pl.when(me_r == h * stride)
        def _():
            part_recv[me] = part_send[i, me_p]

        for step in range(1, n_p):
            part_copy(i, step).start()

    def total_copy(i, step):
        return pltpu.make_async_remote_copy(
            src_ref=total_v.at[i], dst_ref=total_v.at[i],
            send_sem=total_ssem.at[step], recv_sem=total_rsem.at[i],
            device_id=(me_p, peers_r[step]), device_id_type=MESH)

    def add_up(i):
        @pl.when(me_r == order[i] * stride)
        def _():
            others = part_recv.at[pl.ds(0, n_dev - 1)]
            pltpu.make_async_copy(others, others, part_rsem).wait()

            def body(s, totals):
                prompt = group_ref[s]
                piece = part_recv[s].astype(jnp.float32)
                return tuple(
                    total + jnp.where(prompt == p, piece, 0.0) for p, total in enumerate(totals))

            zero = jnp.zeros(part_recv.shape[1:], jnp.float32)
            totals = lax.fori_loop(0, n_dev, body, (zero,) * prompts)
            for p in range(prompts):
                total_v[i, p] = totals[p].astype(jnp.bfloat16)
            for step in range(1, n_r):
                total_copy(i, step).start()

    stores = []

    def store(ref, out):
        copy = pltpu.make_async_copy(ref, out, store_sem.at[len(stores)])
        copy.start()
        stores.append(copy)

    def resp_terms(i):
        h = order[i]
        lanes = lanes_of(h)
        key_sums, value_sums = [], []
        for t in range(tiles):
            depth = (t + 1) * TILE
            query = stacked(query_v, h, t)
            prob = weight_v[h, t, 0:depth] * stat_v[h, t, 3:4]
            dscore = (prob * (dprob_v[h, t, 0:depth] - stat_v[h, t, 4:5])).astype(jnp.bfloat16)
            value_sums.append(dot(prob.astype(jnp.bfloat16), live_grad_v[h, t], NN))
            key_sums.append(dot(dscore, query, NN))
            turned = dot(
                keys_v[0:front + depth, lanes],
                jnp.concatenate([dfront_v[h, t], dscore], 0), TN) * SCALE
            turned = turned.astype(jnp.bfloat16)
            for g in range(GROUP):
                dquery_v[t * TILE:(t + 1) * TILE, (h * GROUP + g) * HD:(h * GROUP + g + 1) * HD] = (
                    turned[:, g * TILE:(g + 1) * TILE].T)
        for t in range(tiles):
            span = slice(t * TILE, (t + 1) * TILE)
            dkey_v[span, lanes] = (
                sum(s[span] for s in key_sums[t:]) * SCALE).astype(jnp.bfloat16)
            dvalue_v[span, lanes] = sum(s[span] for s in value_sums[t:]).astype(jnp.bfloat16)
        cols = pl.ds(h * wide, wide)
        store(dquery_v.at[:, cols], dquery_hbm.at[0, :, cols])

    loads["k"].wait()
    loads["v"].wait()
    resp_scores(0)

    loads["pk"].wait()
    loads["pv"].wait()

    def front_of(q):
        prompt = group_ref[q * n_r + me_r]
        return jnp.concatenate(
            [pkeys_v[prompt].astype(jnp.float32), pvalues_v[prompt].astype(jnp.float32)], 0
        ).astype(jnp.bfloat16)

    for q in range(n_p):
        front_send[q] = front_of(q)
    front_recv[me_p] = front_of(me_p)
    pl.semaphore_wait(barrier, n_dev - 1)

    front_copies = []
    for step in range(1, n_p):
        to = peers_p[step]
        copy = pltpu.make_async_remote_copy(
            src_ref=front_send.at[to], dst_ref=front_recv.at[me_p],
            send_sem=front_ssem.at[step], recv_sem=front_rsem.at[me_p],
            device_id=(to, me_r), device_id_type=MESH)
        copy.start()
        front_copies.append(copy)

    for i in range(1, KVH):
        resp_scores(i)

    for step in range(1, n_p):
        source = peers_p[step]
        pltpu.make_async_remote_copy(
            src_ref=front_send.at[source], dst_ref=front_recv.at[source],
            send_sem=front_ssem.at[step], recv_sem=front_rsem.at[source],
            device_id=(source, me_r), device_id_type=MESH).wait_recv()
    arrived = [front_recv[q].astype(jnp.float32) for q in range(n_p)]
    keys_v[0:front] = jnp.concatenate([a[0:own] for a in arrived], 0).astype(jnp.bfloat16)
    values_v[0:front] = jnp.concatenate([a[own:] for a in arrived], 0).astype(jnp.bfloat16)

    for i in range(KVH):
        front_terms(i)
    resp_terms(0)
    resp_terms(1)
    for i in range(KVH):
        add_up(i)
    resp_terms(2)
    resp_terms(3)
    store(dkey_v, dkey_hbm.at[0])
    store(dvalue_v, dvalue_hbm.at[0])

    for i, h in enumerate(order):
        @pl.when(me_r != h * stride)
        def _():
            total_copy(i, 1).wait_recv()

        total_ref[h] = total_v[i]

    for copy in stores:
        copy.wait()
    for copy in front_copies:
        copy.wait_send()
    for i, h in enumerate(order):
        @pl.when(me_r != h * stride)
        def _():
            part_copy(i, 0).wait_send()

        for step in range(1, n_p):
            part_copy(i, step).wait_send()

        @pl.when(me_r == h * stride)
        def _():
            for step in range(1, n_r):
                total_copy(i, step).wait_send()


def write_out(
    dquery, dkey, dvalue, total, dquery_out, dkey_out, dvalue_out, dpkey, dpvalue,
    dquery_v, dkey_v, dvalue_v, in_sem, out_sem,
):
    moves = []
    cut = dquery.shape[1] // PIECES
    spans = [(dkey, dkey_v, dkey_out, pl.ds(0, dkey.shape[1]))]
    spans.append((dvalue, dvalue_v, dvalue_out, pl.ds(0, dvalue.shape[1])))
    for n in range(PIECES):
        spans.append((dquery, dquery_v, dquery_out, pl.ds(n * cut, cut)))
    for n, (src, mid, dst, rows) in enumerate(spans):
        come = pltpu.make_async_copy(src.at[0, rows], mid.at[rows], in_sem.at[n])
        go = pltpu.make_async_copy(mid.at[rows], dst.at[0, rows], out_sem.at[n])
        come.start()
        moves.append((come, go))
    for come, go in moves:
        come.wait()
        go.start()
    own = dpkey.shape[1]
    for h in range(KVH):
        both = total[h].astype(jnp.float32)
        dpkey[:, :, h * HD:(h + 1) * HD] = both[:, 0:own]
        dpvalue[:, :, h * HD:(h + 1) * HD] = both[:, own:]
    for come, go in moves:
        go.wait()


def shards(n_p, n_r, query, resp_keys, resp_values, prompt_keys, prompt_values, out_grad, group, lengths):
    rows = query.shape[1]
    prompts, own, kvw = prompt_keys.shape
    front = own * n_p
    n_dev = n_p * n_r
    tiles = rows // TILE
    order = (0, 3, 1, 2)
    low = jnp.bfloat16
    vmem = pl.BlockSpec(memory_space=pltpu.VMEM)
    smem = pl.BlockSpec(memory_space=pltpu.SMEM)
    some = pl.BlockSpec(memory_space=pl.ANY)
    hbm = pl.BlockSpec(memory_space=pltpu.HBM)
    dma = pltpu.SemaphoreType.DMA
    like = lambda x, dtype: jax.ShapeDtypeStruct(x.shape, dtype)
    dquery, dkey, dvalue, total = pl.pallas_call(
        functools.partial(kernel, n_p, n_r, order),
        out_shape=(
            like(query, low), like(resp_keys, low), like(resp_values, low),
            jax.ShapeDtypeStruct((KVH, prompts, 2 * own, HD), low),
        ),
        in_specs=[smem, smem] + [hbm] * 6,
        out_specs=(some, some, some, vmem),
        scratch_shapes=[
            pltpu.VMEM((rows, QH * HD), low),
            pltpu.VMEM((rows, QH * HD), low),
            pltpu.VMEM((KVH, tiles, GROUP * TILE, HD), low),
            pltpu.VMEM((front + rows, kvw), low),
            pltpu.VMEM((front + rows, kvw), low),
            pltpu.VMEM((prompts, own, kvw), low),
            pltpu.VMEM((prompts, own, kvw), low),
            pltpu.VMEM((TILE, TILE), jnp.float32),
            pltpu.VMEM((KVH, tiles, rows, GROUP * TILE), jnp.float32),
            pltpu.VMEM((KVH, tiles, rows, GROUP * TILE), jnp.float32),
            pltpu.VMEM((KVH, tiles, 8, GROUP * TILE), jnp.float32),
            pltpu.VMEM((KVH, tiles, front, GROUP * TILE), low),
            pltpu.VMEM((rows, QH * HD), low),
            pltpu.VMEM((rows, kvw), low),
            pltpu.VMEM((rows, kvw), low),
            pltpu.VMEM((n_p, 2 * own, kvw), low),
            pltpu.VMEM((n_p, 2 * own, kvw), low),
            pltpu.VMEM((KVH, n_p, 2 * own, HD), low),
            pltpu.VMEM((n_dev, 2 * own, HD), low),
            pltpu.VMEM((KVH, prompts, 2 * own, HD), low),
            dma((5 + 2 * KVH,)),
            dma((2 + KVH,)),
            dma((n_p,)),
            dma((n_p,)),
            dma((KVH, n_p)),
            dma,
            dma((n_r,)),
            dma((KVH,)),
        ],
        compiler_params=pltpu.CompilerParams(
            collective_id=0, has_side_effects=True, vmem_limit_bytes=60 * 1024 * 1024),
    )(group, lengths, query, out_grad, resp_keys, resp_values, prompt_keys, prompt_values)
    return pl.pallas_call(
        write_out,
        out_shape=(
            like(query, low), like(resp_keys, low), like(resp_values, low),
            like(prompt_keys, jnp.float32), like(prompt_values, jnp.float32),
        ),
        in_specs=[some, some, some, vmem],
        out_specs=(some, some, some, vmem, vmem),
        scratch_shapes=[
            pltpu.VMEM((rows, QH * HD), low),
            pltpu.VMEM((rows, kvw), low),
            pltpu.VMEM((rows, kvw), low),
            dma((2 + PIECES,)),
            dma((2 + PIECES,)),
        ],
        compiler_params=pltpu.CompilerParams(vmem_limit_bytes=60 * 1024 * 1024),
    )(dquery, dkey, dvalue, total)


def solution(mesh):
    return jax.shard_map(
        functools.partial(shards, mesh.shape["prompt"], mesh.shape["resp"]),
        mesh=mesh,
        in_specs=(
            P(("prompt", "resp"), None, None),
            P(("prompt", "resp"), None, None),
            P(("prompt", "resp"), None, None),
            P(None, "prompt", None),
            P(None, "prompt", None),
            P(("prompt", "resp"), None, None),
            P(),
            P(("prompt", "resp")),
        ),
        out_specs=(
            P(("prompt", "resp"), None, None),
            P(("prompt", "resp"), None, None),
            P(("prompt", "resp"), None, None),
            P(None, "prompt", None),
            P(None, "prompt", None),
        ),
        check_vma=False,
    )
```

```python
import functools
import math

import jax
import jax.numpy as jnp
from jax import lax
from jax.experimental import pallas as pl
from jax.experimental.pallas import tpu as pltpu
from jax.sharding import PartitionSpec as P

QH = 16
KVH = 4
HD = 128
GROUP = QH // KVH
TILE = 128
PIECES = 4
MESH = pl.DeviceIdType.MESH
MASKED = -1e30
SCALE = 1.0 / math.sqrt(HD)
NT = (((1,), (1,)), ((), ()))
NN = (((1,), (0,)), ((), ()))
TN = (((0,), (0,)), ((), ()))


def dot(a, b, dims):
    return lax.dot_general(a, b, dims, preferred_element_type=jnp.float32)


def kernel(
    n_p, n_r, order,
    group_ref, length_ref, query_hbm, grad_hbm, rkeys_hbm, rvalues_hbm, pkeys_hbm, pvalues_hbm,
    dquery_hbm, dkey_hbm, dvalue_hbm, total_ref,
    query_v, grad_v, live_grad_v, keys_v, values_v, pkeys_v, pvalues_v,
    bias_v, weight_v, dprob_v, stat_v, dfront_v, dquery_v, dkey_v, dvalue_v,
    front_send, front_recv, part_send, part_recv, total_v,
    load_sem, store_sem, front_ssem, front_rsem, part_ssem, part_rsem, total_ssem, total_rsem,
):
    rows = query_v.shape[0]
    prompts, own = pkeys_v.shape[:2]
    front = own * n_p
    tiles = rows // TILE
    wide = GROUP * HD
    n_dev = n_p * n_r
    me_p = lax.axis_index("prompt")
    me_r = lax.axis_index("resp")
    me = me_p * n_r + me_r
    stride = n_r // KVH
    power = SCALE * math.log2(math.e)

    barrier = pltpu.get_barrier_semaphore()

    def ahead(place, step, size):
        later = place + step
        return jnp.where(later >= size, later - size, later)

    peers_p = [ahead(me_p, step, n_p) for step in range(n_p)]
    peers_r = [ahead(me_r, step, n_r) for step in range(n_r)]
    for to_p in peers_p:
        for to_r in peers_r:
            if to_p is not peers_p[0] or to_r is not peers_r[0]:
                pl.semaphore_signal(
                    barrier, inc=1, device_id=(to_p, to_r), device_id_type=MESH)

    loads = {}
    resp = pl.ds(front, rows)
    wanted = [("k", rkeys_hbm.at[0], keys_v.at[resp])]
    for h in order:
        cols = pl.ds(h * wide, wide)
        wanted.append((("q", h), query_hbm.at[0, :, cols], query_v.at[:, cols]))
        wanted.append((("g", h), grad_hbm.at[0, :, cols], grad_v.at[:, cols]))
        if h == order[0]:
            wanted.append(("v", rvalues_hbm.at[0], values_v.at[resp]))
            wanted.append(("pk", pkeys_hbm, pkeys_v))
            wanted.append(("pv", pvalues_hbm, pvalues_v))
    for n, (name, src, dst) in enumerate(wanted):
        loads[name] = pltpu.make_async_copy(src, dst, load_sem.at[n])
        loads[name].start()

    live = jnp.where(
        lax.broadcasted_iota(jnp.int32, (rows, HD), 0) < length_ref[0], 1.0, 0.0
    ).astype(jnp.bfloat16)
    bias_v[...] = jnp.where(
        lax.broadcasted_iota(jnp.int32, (TILE, TILE), 0)
        <= lax.broadcasted_iota(jnp.int32, (TILE, TILE), 1), 0.0, MASKED)

    def stacked(ref, h, t, start=0, stop=GROUP):
        return jnp.concatenate(
            [ref[t * TILE:(t + 1) * TILE, (h * GROUP + g) * HD:(h * GROUP + g + 1) * HD]
             for g in range(start, stop)], 0)

    def lanes_of(h):
        return slice(h * HD, (h + 1) * HD)

    def resp_scores(i):
        h = order[i]
        lanes = lanes_of(h)
        loads["q", h].wait()
        loads["g", h].wait()
        for t in range(tiles):
            depth = (t + 1) * TILE
            for g in range(0, GROUP, 2):
                query = stacked(query_v, h, t, g, g + 2)
                grad = stacked(grad_v, h, t, g, g + 2) * jnp.concatenate(
                    [live[t * TILE:(t + 1) * TILE]] * 2, 0)
                span = slice(g * TILE, (g + 2) * TILE)
                live_grad_v[h, t, span] = grad
                scores = dot(keys_v[front:front + depth, lanes], query, NT)
                last = scores[depth - TILE:] + jnp.concatenate([bias_v[...]] * 2, 1)
                scores = jnp.concatenate([scores[:depth - TILE], last], 0) if t else last
                top = jnp.max(scores, 0, keepdims=True)
                weights = jnp.exp2((scores - top) * power)
                dprob = dot(values_v[front:front + depth, lanes], grad, NT)
                weight_v[h, t, 0:depth, span] = weights
                dprob_v[h, t, 0:depth, span] = dprob
                stat_v[h, t, 0:1, span] = top
                stat_v[h, t, 1:2, span] = jnp.sum(weights, 0, keepdims=True)
                stat_v[h, t, 2:3, span] = jnp.sum(weights * dprob, 0, keepdims=True)

    def part_copy(i, step):
        to = peers_p[step]
        return pltpu.make_async_remote_copy(
            src_ref=part_send.at[i, to], dst_ref=part_recv.at[me],
            send_sem=part_ssem.at[i, step], recv_sem=part_rsem,
            device_id=(to, order[i] * stride), device_id_type=MESH)

    def front_terms(i):
        h = order[i]
        lanes = lanes_of(h)
        front_key, front_value = 0.0, 0.0
        for t in range(tiles):
            query = stacked(query_v, h, t)
            grad = live_grad_v[h, t]
            resp_top = stat_v[h, t, 0:1]
            scores = dot(keys_v[0:front, lanes], query, NT)
            dprob = dot(values_v[0:front, lanes], grad, NT)
            top = jnp.maximum(resp_top, jnp.max(scores, 0, keepdims=True))
            shrink = jnp.exp2((resp_top - top) * power)
            weights = jnp.exp2((scores - top) * power)
            inverse = 1.0 / (shrink * stat_v[h, t, 1:2] + jnp.sum(weights, 0, keepdims=True))
            factor = shrink * inverse
            prob = weights * inverse
            delta = factor * stat_v[h, t, 2:3] + jnp.sum(prob * dprob, 0, keepdims=True)
            dscore = (prob * (dprob - delta)).astype(jnp.bfloat16)
            dfront_v[h, t] = dscore
            stat_v[h, t, 3:4] = factor
            stat_v[h, t, 4:5] = delta
            front_value += dot(prob.astype(jnp.bfloat16), grad, NN)
            front_key += dot(dscore, query, NN)
        front_key = front_key * SCALE
        for q in range(n_p):
            part_send[i, q] = jnp.concatenate(
                [front_key[q * own:(q + 1) * own], front_value[q * own:(q + 1) * own]], 0
            ).astype(jnp.bfloat16)

        @pl.when(me_r != h * stride)
        def _():
            part_copy(i, 0).start()

        @pl.when(me_r == h * stride)
        def _():
            part_recv[me] = part_send[i, me_p]

        for step in range(1, n_p):
            part_copy(i, step).start()

    def total_copy(i, step):
        return pltpu.make_async_remote_copy(
            src_ref=total_v.at[i], dst_ref=total_v.at[i],
            send_sem=total_ssem.at[step], recv_sem=total_rsem.at[i],
            device_id=(me_p, peers_r[step]), device_id_type=MESH)

    def add_up(i):
        @pl.when(me_r == order[i] * stride)
        def _():
            others = part_recv.at[pl.ds(0, n_dev - 1)]
            pltpu.make_async_copy(others, others, part_rsem).wait()

            def body(s, totals):
                prompt = group_ref[s]
                piece = part_recv[s].astype(jnp.float32)
                return tuple(
                    total + jnp.where(prompt == p, piece, 0.0) for p, total in enumerate(totals))

            zero = jnp.zeros(part_recv.shape[1:], jnp.float32)
            totals = lax.fori_loop(0, n_dev, body, (zero,) * prompts)
            for p in range(prompts):
                total_v[i, p] = totals[p].astype(jnp.bfloat16)
            for step in range(1, n_r):
                total_copy(i, step).start()

    stores = []

    def store(ref, out):
        copy = pltpu.make_async_copy(ref, out, store_sem.at[len(stores)])
        copy.start()
        stores.append(copy)

    def resp_terms(i):
        h = order[i]
        lanes = lanes_of(h)
        key_sums, value_sums = [], []
        for t in range(tiles):
            depth = (t + 1) * TILE
            query = stacked(query_v, h, t)
            prob = weight_v[h, t, 0:depth] * stat_v[h, t, 3:4]
            dscore = (prob * (dprob_v[h, t, 0:depth] - stat_v[h, t, 4:5])).astype(jnp.bfloat16)
            value_sums.append(dot(prob.astype(jnp.bfloat16), live_grad_v[h, t], NN))
            key_sums.append(dot(dscore, query, NN))
            turned = dot(
                keys_v[0:front + depth, lanes],
                jnp.concatenate([dfront_v[h, t], dscore], 0), TN) * SCALE
            turned = turned.astype(jnp.bfloat16)
            for g in range(GROUP):
                dquery_v[t * TILE:(t + 1) * TILE, (h * GROUP + g) * HD:(h * GROUP + g + 1) * HD] = (
                    turned[:, g * TILE:(g + 1) * TILE].T)
        for t in range(tiles):
            span = slice(t * TILE, (t + 1) * TILE)
            dkey_v[span, lanes] = (
                sum(s[span] for s in key_sums[t:]) * SCALE).astype(jnp.bfloat16)
            dvalue_v[span, lanes] = sum(s[span] for s in value_sums[t:]).astype(jnp.bfloat16)
        cols = pl.ds(h * wide, wide)
        store(dquery_v.at[:, cols], dquery_hbm.at[0, :, cols])

    loads["k"].wait()
    loads["v"].wait()
    resp_scores(0)

    loads["pk"].wait()
    loads["pv"].wait()

    def front_of(q):
        prompt = group_ref[q * n_r + me_r]
        return jnp.concatenate(
            [pkeys_v[prompt].astype(jnp.float32), pvalues_v[prompt].astype(jnp.float32)], 0
        ).astype(jnp.bfloat16)

    for q in range(n_p):
        front_send[q] = front_of(q)
    front_recv[me_p] = front_of(me_p)
    pl.semaphore_wait(barrier, n_dev - 1)

    front_copies = []
    for step in range(1, n_p):
        to = peers_p[step]
        copy = pltpu.make_async_remote_copy(
            src_ref=front_send.at[to], dst_ref=front_recv.at[me_p],
            send_sem=front_ssem.at[step], recv_sem=front_rsem.at[me_p],
            device_id=(to, me_r), device_id_type=MESH)
        copy.start()
        front_copies.append(copy)

    for i in range(1, KVH):
        resp_scores(i)

    for step in range(1, n_p):
        source = peers_p[step]
        pltpu.make_async_remote_copy(
            src_ref=front_send.at[source], dst_ref=front_recv.at[source],
            send_sem=front_ssem.at[step], recv_sem=front_rsem.at[source],
            device_id=(source, me_r), device_id_type=MESH).wait_recv()
    arrived = [front_recv[q].astype(jnp.float32) for q in range(n_p)]
    keys_v[0:front] = jnp.concatenate([a[0:own] for a in arrived], 0).astype(jnp.bfloat16)
    values_v[0:front] = jnp.concatenate([a[own:] for a in arrived], 0).astype(jnp.bfloat16)

    for i in range(KVH):
        front_terms(i)
    resp_terms(0)
    add_up(0)
    add_up(1)
    resp_terms(1)
    add_up(2)
    add_up(3)
    resp_terms(2)
    resp_terms(3)
    store(dkey_v, dkey_hbm.at[0])
    store(dvalue_v, dvalue_hbm.at[0])

    for i, h in enumerate(order):
        @pl.when(me_r != h * stride)
        def _():
            total_copy(i, 1).wait_recv()

        total_ref[h] = total_v[i]

    for copy in stores:
        copy.wait()
    for copy in front_copies:
        copy.wait_send()
    for i, h in enumerate(order):
        @pl.when(me_r != h * stride)
        def _():
            part_copy(i, 0).wait_send()

        for step in range(1, n_p):
            part_copy(i, step).wait_send()

        @pl.when(me_r == h * stride)
        def _():
            for step in range(1, n_r):
                total_copy(i, step).wait_send()


def write_out(dquery, dkey, dvalue, total, dquery_out, dkey_out, dvalue_out, dpkey, dpvalue, sem):
    copies = []
    cut = dquery.shape[1] // PIECES
    spans = [(dquery, dquery_out, pl.ds(n * cut, cut)) for n in range(PIECES)]
    spans.append((dkey, dkey_out, pl.ds(0, dkey.shape[1])))
    spans.append((dvalue, dvalue_out, pl.ds(0, dvalue.shape[1])))
    for n, (src, dst, rows) in enumerate(spans):
        copies.append(pltpu.make_async_copy(src.at[0, rows], dst.at[0, rows], sem.at[n]))
        copies[-1].start()
    own = dpkey.shape[1]
    for h in range(KVH):
        both = total[h].astype(jnp.float32)
        dpkey[:, :, h * HD:(h + 1) * HD] = both[:, 0:own]
        dpvalue[:, :, h * HD:(h + 1) * HD] = both[:, own:]
    for copy in copies:
        copy.wait()


def shards(n_p, n_r, query, resp_keys, resp_values, prompt_keys, prompt_values, out_grad, group, lengths):
    rows = query.shape[1]
    prompts, own, kvw = prompt_keys.shape
    front = own * n_p
    n_dev = n_p * n_r
    tiles = rows // TILE
    order = (0, 3, 1, 2)
    low = jnp.bfloat16
    vmem = pl.BlockSpec(memory_space=pltpu.VMEM)
    smem = pl.BlockSpec(memory_space=pltpu.SMEM)
    some = pl.BlockSpec(memory_space=pl.ANY)
    hbm = pl.BlockSpec(memory_space=pltpu.HBM)
    dma = pltpu.SemaphoreType.DMA
    like = lambda x, dtype: jax.ShapeDtypeStruct(x.shape, dtype)
    dquery, dkey, dvalue, total = pl.pallas_call(
        functools.partial(kernel, n_p, n_r, order),
        out_shape=(
            pltpu.VMEM(query.shape, low), pltpu.VMEM(resp_keys.shape, low),
            pltpu.VMEM(resp_values.shape, low), pltpu.VMEM((KVH, prompts, 2 * own, HD), low),
        ),
        in_specs=[smem, smem] + [hbm] * 6,
        out_specs=(some, some, some, vmem),
        scratch_shapes=[
            pltpu.VMEM((rows, QH * HD), low),
            pltpu.VMEM((rows, QH * HD), low),
            pltpu.VMEM((KVH, tiles, GROUP * TILE, HD), low),
            pltpu.VMEM((front + rows, kvw), low),
            pltpu.VMEM((front + rows, kvw), low),
            pltpu.VMEM((prompts, own, kvw), low),
            pltpu.VMEM((prompts, own, kvw), low),
            pltpu.VMEM((TILE, TILE), jnp.float32),
            pltpu.VMEM((KVH, tiles, rows, GROUP * TILE), jnp.float32),
            pltpu.VMEM((KVH, tiles, rows, GROUP * TILE), jnp.float32),
            pltpu.VMEM((KVH, tiles, 8, GROUP * TILE), jnp.float32),
            pltpu.VMEM((KVH, tiles, front, GROUP * TILE), low),
            pltpu.VMEM((rows, QH * HD), low),
            pltpu.VMEM((rows, kvw), low),
            pltpu.VMEM((rows, kvw), low),
            pltpu.VMEM((n_p, 2 * own, kvw), low),
            pltpu.VMEM((n_p, 2 * own, kvw), low),
            pltpu.VMEM((KVH, n_p, 2 * own, HD), low),
            pltpu.VMEM((n_dev, 2 * own, HD), low),
            pltpu.VMEM((KVH, prompts, 2 * own, HD), low),
            dma((5 + 2 * KVH,)),
            dma((2 + KVH,)),
            dma((n_p,)),
            dma((n_p,)),
            dma((KVH, n_p)),
            dma,
            dma((n_r,)),
            dma((KVH,)),
        ],
        compiler_params=pltpu.CompilerParams(
            collective_id=0, has_side_effects=True, vmem_limit_bytes=60 * 1024 * 1024),
    )(group, lengths, query, out_grad, resp_keys, resp_values, prompt_keys, prompt_values)
    return pl.pallas_call(
        write_out,
        out_shape=(
            like(query, low), like(resp_keys, low), like(resp_values, low),
            like(prompt_keys, jnp.float32), like(prompt_values, jnp.float32),
        ),
        in_specs=[some, some, some, vmem],
        out_specs=(some, some, some, vmem, vmem),
        scratch_shapes=[dma((2 + PIECES,))],
        compiler_params=pltpu.CompilerParams(vmem_limit_bytes=16 * 1024 * 1024),
    )(dquery, dkey, dvalue, total)


def solution(mesh):
    return jax.shard_map(
        functools.partial(shards, mesh.shape["prompt"], mesh.shape["resp"]),
        mesh=mesh,
        in_specs=(
            P(("prompt", "resp"), None, None),
            P(("prompt", "resp"), None, None),
            P(("prompt", "resp"), None, None),
            P(None, "prompt", None),
            P(None, "prompt", None),
            P(("prompt", "resp"), None, None),
            P(),
            P(("prompt", "resp")),
        ),
        out_specs=(
            P(("prompt", "resp"), None, None),
            P(("prompt", "resp"), None, None),
            P(("prompt", "resp"), None, None),
            P(None, "prompt", None),
            P(None, "prompt", None),
        ),
        check_vma=False,
    )
```

```python
import functools
import math

import jax
import jax.numpy as jnp
from jax import lax
from jax.experimental import pallas as pl
from jax.experimental.pallas import tpu as pltpu
from jax.sharding import PartitionSpec as P

QH = 16
KVH = 4
HD = 128
GROUP = QH // KVH
TILE = 128
PIECES = 4
MESH = pl.DeviceIdType.MESH
MASKED = -1e30
SCALE = 1.0 / math.sqrt(HD)
NT = (((1,), (1,)), ((), ()))
NN = (((1,), (0,)), ((), ()))
TN = (((0,), (0,)), ((), ()))


def dot(a, b, dims):
    return lax.dot_general(a, b, dims, preferred_element_type=jnp.float32)


def kernel(
    n_p, n_r, order,
    group_ref, length_ref, query_hbm, grad_hbm, rkeys_hbm, rvalues_hbm, pkeys_hbm, pvalues_hbm,
    dquery_hbm, dkey_hbm, dvalue_hbm, total_ref,
    query_v, grad_v, live_grad_v, keys_v, values_v, pkeys_v, pvalues_v,
    bias_v, weight_v, dprob_v, stat_v, dfront_v, dquery_v, dkey_v, dvalue_v,
    front_send, front_recv, part_send, part_recv, total_v,
    load_sem, store_sem, front_ssem, front_rsem, part_ssem, part_rsem, total_ssem, total_rsem,
):
    rows = query_v.shape[0]
    prompts, own = pkeys_v.shape[:2]
    front = own * n_p
    tiles = rows // TILE
    wide = GROUP * HD
    n_dev = n_p * n_r
    me_p = lax.axis_index("prompt")
    me_r = lax.axis_index("resp")
    me = me_p * n_r + me_r
    stride = n_r // KVH
    power = SCALE * math.log2(math.e)

    barrier = pltpu.get_barrier_semaphore()

    def ahead(place, step, size):
        later = place + step
        return jnp.where(later >= size, later - size, later)

    peers_p = [ahead(me_p, step, n_p) for step in range(n_p)]
    peers_r = [ahead(me_r, step, n_r) for step in range(n_r)]
    for to_p in peers_p:
        for to_r in peers_r:
            if to_p is not peers_p[0] or to_r is not peers_r[0]:
                pl.semaphore_signal(
                    barrier, inc=1, device_id=(to_p, to_r), device_id_type=MESH)

    loads = {}
    resp = pl.ds(front, rows)
    wanted = [("k", rkeys_hbm.at[0], keys_v.at[resp])]
    for h in order:
        cols = pl.ds(h * wide, wide)
        wanted.append((("q", h), query_hbm.at[0, :, cols], query_v.at[:, cols]))
        wanted.append((("g", h), grad_hbm.at[0, :, cols], grad_v.at[:, cols]))
        if h == order[0]:
            wanted.append(("v", rvalues_hbm.at[0], values_v.at[resp]))
            wanted.append(("pk", pkeys_hbm, pkeys_v))
            wanted.append(("pv", pvalues_hbm, pvalues_v))
    for n, (name, src, dst) in enumerate(wanted):
        loads[name] = pltpu.make_async_copy(src, dst, load_sem.at[n])
        loads[name].start()

    live = jnp.where(
        lax.broadcasted_iota(jnp.int32, (rows, HD), 0) < length_ref[0], 1.0, 0.0
    ).astype(jnp.bfloat16)
    bias_v[...] = jnp.where(
        lax.broadcasted_iota(jnp.int32, (TILE, TILE), 0)
        <= lax.broadcasted_iota(jnp.int32, (TILE, TILE), 1), 0.0, MASKED)

    def stacked(ref, h, t, start=0, stop=GROUP):
        return jnp.concatenate(
            [ref[t * TILE:(t + 1) * TILE, (h * GROUP + g) * HD:(h * GROUP + g + 1) * HD]
             for g in range(start, stop)], 0)

    def lanes_of(h):
        return slice(h * HD, (h + 1) * HD)

    def resp_scores(i):
        h = order[i]
        lanes = lanes_of(h)
        loads["q", h].wait()
        loads["g", h].wait()
        for t in range(tiles):
            depth = (t + 1) * TILE
            for g in range(0, GROUP, 2):
                query = stacked(query_v, h, t, g, g + 2)
                grad = stacked(grad_v, h, t, g, g + 2) * jnp.concatenate(
                    [live[t * TILE:(t + 1) * TILE]] * 2, 0)
                span = slice(g * TILE, (g + 2) * TILE)
                live_grad_v[h, t, span] = grad
                scores = dot(keys_v[front:front + depth, lanes], query, NT)
                last = scores[depth - TILE:] + jnp.concatenate([bias_v[...]] * 2, 1)
                scores = jnp.concatenate([scores[:depth - TILE], last], 0) if t else last
                top = jnp.max(scores, 0, keepdims=True)
                weights = jnp.exp2((scores - top) * power)
                dprob = dot(values_v[front:front + depth, lanes], grad, NT)
                weight_v[h, t, 0:depth, span] = weights
                dprob_v[h, t, 0:depth, span] = dprob
                stat_v[h, t, 0:1, span] = top
                stat_v[h, t, 1:2, span] = jnp.sum(weights, 0, keepdims=True)
                stat_v[h, t, 2:3, span] = jnp.sum(weights * dprob, 0, keepdims=True)

    def part_copy(i, step):
        to = peers_p[step]
        return pltpu.make_async_remote_copy(
            src_ref=part_send.at[i, to], dst_ref=part_recv.at[me],
            send_sem=part_ssem.at[i, step], recv_sem=part_rsem,
            device_id=(to, order[i] * stride), device_id_type=MESH)

    def front_terms(i):
        h = order[i]
        lanes = lanes_of(h)
        front_key, front_value = 0.0, 0.0
        for t in range(tiles):
            query = stacked(query_v, h, t)
            grad = live_grad_v[h, t]
            resp_top = stat_v[h, t, 0:1]
            scores = dot(keys_v[0:front, lanes], query, NT)
            dprob = dot(values_v[0:front, lanes], grad, NT)
            top = jnp.maximum(resp_top, jnp.max(scores, 0, keepdims=True))
            shrink = jnp.exp2((resp_top - top) * power)
            weights = jnp.exp2((scores - top) * power)
            inverse = 1.0 / (shrink * stat_v[h, t, 1:2] + jnp.sum(weights, 0, keepdims=True))
            factor = shrink * inverse
            prob = weights * inverse
            delta = factor * stat_v[h, t, 2:3] + jnp.sum(prob * dprob, 0, keepdims=True)
            dscore = (prob * (dprob - delta)).astype(jnp.bfloat16)
            dfront_v[h, t] = dscore
            stat_v[h, t, 3:4] = factor
            stat_v[h, t, 4:5] = delta
            front_value += dot(prob.astype(jnp.bfloat16), grad, NN)
            front_key += dot(dscore, query, NN)
        front_key = front_key * SCALE
        for q in range(n_p):
            part_send[i, q] = jnp.concatenate(
                [front_key[q * own:(q + 1) * own], front_value[q * own:(q + 1) * own]], 0
            ).astype(jnp.bfloat16)

        @pl.when(me_r != h * stride)
        def _():
            part_copy(i, 0).start()

        @pl.when(me_r == h * stride)
        def _():
            part_recv[me] = part_send[i, me_p]

        for step in range(1, n_p):
            part_copy(i, step).start()

    def total_copy(i, step):
        return pltpu.make_async_remote_copy(
            src_ref=total_v.at[i], dst_ref=total_v.at[i],
            send_sem=total_ssem.at[step], recv_sem=total_rsem.at[i],
            device_id=(me_p, peers_r[step]), device_id_type=MESH)

    def add_up(i):
        @pl.when(me_r == order[i] * stride)
        def _():
            others = part_recv.at[pl.ds(0, n_dev - 1)]
            pltpu.make_async_copy(others, others, part_rsem).wait()

            def body(s, totals):
                prompt = group_ref[s]
                piece = part_recv[s].astype(jnp.float32)
                return tuple(
                    total + jnp.where(prompt == p, piece, 0.0) for p, total in enumerate(totals))

            zero = jnp.zeros(part_recv.shape[1:], jnp.float32)
            totals = lax.fori_loop(0, n_dev, body, (zero,) * prompts)
            for p in range(prompts):
                total_v[i, p] = totals[p].astype(jnp.bfloat16)
            for step in range(1, n_r):
                total_copy(i, step).start()

    stores = []

    def store(ref, out):
        copy = pltpu.make_async_copy(ref, out, store_sem.at[len(stores)])
        copy.start()
        stores.append(copy)

    def resp_terms(i):
        h = order[i]
        lanes = lanes_of(h)
        key_sums, value_sums = [], []
        for t in range(tiles):
            depth = (t + 1) * TILE
            query = stacked(query_v, h, t)
            prob = weight_v[h, t, 0:depth] * stat_v[h, t, 3:4]
            dscore = (prob * (dprob_v[h, t, 0:depth] - stat_v[h, t, 4:5])).astype(jnp.bfloat16)
            value_sums.append(dot(prob.astype(jnp.bfloat16), live_grad_v[h, t], NN))
            key_sums.append(dot(dscore, query, NN))
            turned = dot(
                keys_v[0:front + depth, lanes],
                jnp.concatenate([dfront_v[h, t], dscore], 0), TN) * SCALE
            turned = turned.astype(jnp.bfloat16)
            for g in range(GROUP):
                dquery_v[t * TILE:(t + 1) * TILE, (h * GROUP + g) * HD:(h * GROUP + g + 1) * HD] = (
                    turned[:, g * TILE:(g + 1) * TILE].T)
        for t in range(tiles):
            span = slice(t * TILE, (t + 1) * TILE)
            dkey_v[span, lanes] = (
                sum(s[span] for s in key_sums[t:]) * SCALE).astype(jnp.bfloat16)
            dvalue_v[span, lanes] = sum(s[span] for s in value_sums[t:]).astype(jnp.bfloat16)
        cols = pl.ds(h * wide, wide)
        store(dquery_v.at[:, cols], dquery_hbm.at[0, :, cols])

    loads["k"].wait()
    loads["v"].wait()
    resp_scores(0)

    loads["pk"].wait()
    loads["pv"].wait()

    def front_of(q):
        prompt = group_ref[q * n_r + me_r]
        return jnp.concatenate(
            [pkeys_v[prompt].astype(jnp.float32), pvalues_v[prompt].astype(jnp.float32)], 0
        ).astype(jnp.bfloat16)

    for q in range(n_p):
        front_send[q] = front_of(q)
    front_recv[me_p] = front_of(me_p)
    pl.semaphore_wait(barrier, n_dev - 1)

    front_copies = []
    for step in range(1, n_p):
        to = peers_p[step]
        copy = pltpu.make_async_remote_copy(
            src_ref=front_send.at[to], dst_ref=front_recv.at[me_p],
            send_sem=front_ssem.at[step], recv_sem=front_rsem.at[me_p],
            device_id=(to, me_r), device_id_type=MESH)
        copy.start()
        front_copies.append(copy)

    resp_scores(1)

    for step in range(1, n_p):
        source = peers_p[step]
        pltpu.make_async_remote_copy(
            src_ref=front_send.at[source], dst_ref=front_recv.at[source],
            send_sem=front_ssem.at[step], recv_sem=front_rsem.at[source],
            device_id=(source, me_r), device_id_type=MESH).wait_recv()
    arrived = [front_recv[q].astype(jnp.float32) for q in range(n_p)]
    keys_v[0:front] = jnp.concatenate([a[0:own] for a in arrived], 0).astype(jnp.bfloat16)
    values_v[0:front] = jnp.concatenate([a[own:] for a in arrived], 0).astype(jnp.bfloat16)

    front_terms(0)
    front_terms(1)
    resp_scores(2)
    front_terms(2)
    resp_scores(3)
    front_terms(3)
    add_up(0)
    add_up(1)
    resp_terms(0)
    add_up(2)
    add_up(3)
    resp_terms(1)
    resp_terms(2)
    resp_terms(3)
    store(dkey_v, dkey_hbm.at[0])
    store(dvalue_v, dvalue_hbm.at[0])

    for i, h in enumerate(order):
        @pl.when(me_r != h * stride)
        def _():
            total_copy(i, 1).wait_recv()

        total_ref[h] = total_v[i]

    for copy in stores:
        copy.wait()
    for copy in front_copies:
        copy.wait_send()
    for i, h in enumerate(order):
        @pl.when(me_r != h * stride)
        def _():
            part_copy(i, 0).wait_send()

        for step in range(1, n_p):
            part_copy(i, step).wait_send()

        @pl.when(me_r == h * stride)
        def _():
            for step in range(1, n_r):
                total_copy(i, step).wait_send()


def write_out(dquery, dkey, dvalue, total, dquery_out, dkey_out, dvalue_out, dpkey, dpvalue, sem):
    copies = []
    cut = dquery.shape[1] // PIECES
    spans = [(dquery, dquery_out, pl.ds(n * cut, cut)) for n in range(PIECES)]
    spans.append((dkey, dkey_out, pl.ds(0, dkey.shape[1])))
    spans.append((dvalue, dvalue_out, pl.ds(0, dvalue.shape[1])))
    for n, (src, dst, rows) in enumerate(spans):
        copies.append(pltpu.make_async_copy(src.at[0, rows], dst.at[0, rows], sem.at[n]))
        copies[-1].start()
    own = dpkey.shape[1]
    for h in range(KVH):
        both = total[h].astype(jnp.float32)
        dpkey[:, :, h * HD:(h + 1) * HD] = both[:, 0:own]
        dpvalue[:, :, h * HD:(h + 1) * HD] = both[:, own:]
    for copy in copies:
        copy.wait()


def shards(n_p, n_r, query, resp_keys, resp_values, prompt_keys, prompt_values, out_grad, group, lengths):
    rows = query.shape[1]
    prompts, own, kvw = prompt_keys.shape
    front = own * n_p
    n_dev = n_p * n_r
    tiles = rows // TILE
    order = (0, 3, 1, 2)
    low = jnp.bfloat16
    vmem = pl.BlockSpec(memory_space=pltpu.VMEM)
    smem = pl.BlockSpec(memory_space=pltpu.SMEM)
    some = pl.BlockSpec(memory_space=pl.ANY)
    hbm = pl.BlockSpec(memory_space=pltpu.HBM)
    dma = pltpu.SemaphoreType.DMA
    like = lambda x, dtype: jax.ShapeDtypeStruct(x.shape, dtype)
    dquery, dkey, dvalue, total = pl.pallas_call(
        functools.partial(kernel, n_p, n_r, order),
        out_shape=(
            pltpu.VMEM(query.shape, low), pltpu.VMEM(resp_keys.shape, low),
            pltpu.VMEM(resp_values.shape, low), pltpu.VMEM((KVH, prompts, 2 * own, HD), low),
        ),
        in_specs=[smem, smem] + [hbm] * 6,
        out_specs=(some, some, some, vmem),
        scratch_shapes=[
            pltpu.VMEM((rows, QH * HD), low),
            pltpu.VMEM((rows, QH * HD), low),
            pltpu.VMEM((KVH, tiles, GROUP * TILE, HD), low),
            pltpu.VMEM((front + rows, kvw), low),
            pltpu.VMEM((front + rows, kvw), low),
            pltpu.VMEM((prompts, own, kvw), low),
            pltpu.VMEM((prompts, own, kvw), low),
            pltpu.VMEM((TILE, TILE), jnp.float32),
            pltpu.VMEM((KVH, tiles, rows, GROUP * TILE), jnp.float32),
            pltpu.VMEM((KVH, tiles, rows, GROUP * TILE), jnp.float32),
            pltpu.VMEM((KVH, tiles, 8, GROUP * TILE), jnp.float32),
            pltpu.VMEM((KVH, tiles, front, GROUP * TILE), low),
            pltpu.VMEM((rows, QH * HD), low),
            pltpu.VMEM((rows, kvw), low),
            pltpu.VMEM((rows, kvw), low),
            pltpu.VMEM((n_p, 2 * own, kvw), low),
            pltpu.VMEM((n_p, 2 * own, kvw), low),
            pltpu.VMEM((KVH, n_p, 2 * own, HD), low),
            pltpu.VMEM((n_dev, 2 * own, HD), low),
            pltpu.VMEM((KVH, prompts, 2 * own, HD), low),
            dma((5 + 2 * KVH,)),
            dma((2 + KVH,)),
            dma((n_p,)),
            dma((n_p,)),
            dma((KVH, n_p)),
            dma,
            dma((n_r,)),
            dma((KVH,)),
        ],
        compiler_params=pltpu.CompilerParams(
            collective_id=0, has_side_effects=True, vmem_limit_bytes=60 * 1024 * 1024),
    )(group, lengths, query, out_grad, resp_keys, resp_values, prompt_keys, prompt_values)
    return pl.pallas_call(
        write_out,
        out_shape=(
            like(query, low), like(resp_keys, low), like(resp_values, low),
            like(prompt_keys, jnp.float32), like(prompt_values, jnp.float32),
        ),
        in_specs=[some, some, some, vmem],
        out_specs=(some, some, some, vmem, vmem),
        scratch_shapes=[dma((2 + PIECES,))],
        compiler_params=pltpu.CompilerParams(vmem_limit_bytes=16 * 1024 * 1024),
    )(dquery, dkey, dvalue, total)


def solution(mesh):
    return jax.shard_map(
        functools.partial(shards, mesh.shape["prompt"], mesh.shape["resp"]),
        mesh=mesh,
        in_specs=(
            P(("prompt", "resp"), None, None),
            P(("prompt", "resp"), None, None),
            P(("prompt", "resp"), None, None),
            P(None, "prompt", None),
            P(None, "prompt", None),
            P(("prompt", "resp"), None, None),
            P(),
            P(("prompt", "resp")),
        ),
        out_specs=(
            P(("prompt", "resp"), None, None),
            P(("prompt", "resp"), None, None),
            P(("prompt", "resp"), None, None),
            P(None, "prompt", None),
            P(None, "prompt", None),
        ),
        check_vma=False,
    )
```

```python
import functools
import math

import jax
import jax.numpy as jnp
from jax import lax
from jax.experimental import pallas as pl
from jax.experimental.pallas import tpu as pltpu
from jax.sharding import PartitionSpec as P

QH = 16
KVH = 4
HD = 128
GROUP = QH // KVH
TILE = 128
PIECES = 4
EARLY = 2
MESH = pl.DeviceIdType.MESH
MASKED = -1e30
SCALE = 1.0 / math.sqrt(HD)
NT = (((1,), (1,)), ((), ()))
NN = (((1,), (0,)), ((), ()))
TN = (((0,), (0,)), ((), ()))


def dot(a, b, dims):
    return lax.dot_general(a, b, dims, preferred_element_type=jnp.float32)


def kernel(
    n_p, n_r, order,
    group_ref, length_ref, query_hbm, grad_hbm, rkeys_hbm, rvalues_hbm, pkeys_hbm, pvalues_hbm,
    dquery_hbm, dkey_hbm, dvalue_hbm, total_ref,
    query_v, grad_v, live_grad_v, keys_v, values_v, pkeys_v, pvalues_v,
    bias_v, weight_v, dprob_v, stat_v, dfront_v, dscore_v, dquery_v, dkey_v, dvalue_v,
    front_send, front_recv, part_send, part_recv, total_v,
    load_sem, store_sem, front_ssem, front_rsem, part_ssem, part_rsem, total_ssem, total_rsem,
):
    rows = query_v.shape[0]
    prompts, own = pkeys_v.shape[:2]
    front = own * n_p
    tiles = rows // TILE
    wide = GROUP * HD
    n_dev = n_p * n_r
    me_p = lax.axis_index("prompt")
    me_r = lax.axis_index("resp")
    me = me_p * n_r + me_r
    stride = n_r // KVH
    power = SCALE * math.log2(math.e)

    barrier = pltpu.get_barrier_semaphore()

    def ahead(place, step, size):
        later = place + step
        return jnp.where(later >= size, later - size, later)

    peers_p = [ahead(me_p, step, n_p) for step in range(n_p)]
    peers_r = [ahead(me_r, step, n_r) for step in range(n_r)]
    for to_p in peers_p:
        for to_r in peers_r:
            if to_p is not peers_p[0] or to_r is not peers_r[0]:
                pl.semaphore_signal(
                    barrier, inc=1, device_id=(to_p, to_r), device_id_type=MESH)

    loads = {}
    resp = pl.ds(front, rows)
    wanted = [("k", rkeys_hbm.at[0], keys_v.at[resp])]
    for h in order:
        cols = pl.ds(h * wide, wide)
        wanted.append((("q", h), query_hbm.at[0, :, cols], query_v.at[:, cols]))
        wanted.append((("g", h), grad_hbm.at[0, :, cols], grad_v.at[:, cols]))
        if h == order[0]:
            wanted.append(("v", rvalues_hbm.at[0], values_v.at[resp]))
            wanted.append(("pk", pkeys_hbm, pkeys_v))
            wanted.append(("pv", pvalues_hbm, pvalues_v))
    for n, (name, src, dst) in enumerate(wanted):
        loads[name] = pltpu.make_async_copy(src, dst, load_sem.at[n])
        loads[name].start()

    live = jnp.where(
        lax.broadcasted_iota(jnp.int32, (rows, HD), 0) < length_ref[0], 1.0, 0.0
    ).astype(jnp.bfloat16)
    bias_v[...] = jnp.where(
        lax.broadcasted_iota(jnp.int32, (TILE, TILE), 0)
        <= lax.broadcasted_iota(jnp.int32, (TILE, TILE), 1), 0.0, MASKED)

    def stacked(ref, h, t, start=0, stop=GROUP):
        return jnp.concatenate(
            [ref[t * TILE:(t + 1) * TILE, (h * GROUP + g) * HD:(h * GROUP + g + 1) * HD]
             for g in range(start, stop)], 0)

    def lanes_of(h):
        return slice(h * HD, (h + 1) * HD)

    def resp_scores(i):
        h = order[i]
        lanes = lanes_of(h)
        loads["q", h].wait()
        loads["g", h].wait()
        for t in range(tiles):
            depth = (t + 1) * TILE
            for g in range(0, GROUP, 2):
                query = stacked(query_v, h, t, g, g + 2)
                grad = stacked(grad_v, h, t, g, g + 2) * jnp.concatenate(
                    [live[t * TILE:(t + 1) * TILE]] * 2, 0)
                span = slice(g * TILE, (g + 2) * TILE)
                live_grad_v[h, t, span] = grad
                scores = dot(keys_v[front:front + depth, lanes], query, NT)
                last = scores[depth - TILE:] + jnp.concatenate([bias_v[...]] * 2, 1)
                scores = jnp.concatenate([scores[:depth - TILE], last], 0) if t else last
                top = jnp.max(scores, 0, keepdims=True)
                weights = jnp.exp2((scores - top) * power)
                dprob = dot(values_v[front:front + depth, lanes], grad, NT)
                weight_v[h, t, 0:depth, span] = weights
                dprob_v[h, t, 0:depth, span] = dprob
                stat_v[h, t, 0:1, span] = top
                stat_v[h, t, 1:2, span] = jnp.sum(weights, 0, keepdims=True)
                stat_v[h, t, 2:3, span] = jnp.sum(weights * dprob, 0, keepdims=True)

    def part_copy(i, step):
        to = peers_p[step]
        return pltpu.make_async_remote_copy(
            src_ref=part_send.at[i, to], dst_ref=part_recv.at[me],
            send_sem=part_ssem.at[i, step], recv_sem=part_rsem,
            device_id=(to, order[i] * stride), device_id_type=MESH)

    def front_terms(i):
        h = order[i]
        lanes = lanes_of(h)
        front_key, front_value = 0.0, 0.0
        for t in range(tiles):
            query = stacked(query_v, h, t)
            grad = live_grad_v[h, t]
            resp_top = stat_v[h, t, 0:1]
            scores = dot(keys_v[0:front, lanes], query, NT)
            dprob = dot(values_v[0:front, lanes], grad, NT)
            top = jnp.maximum(resp_top, jnp.max(scores, 0, keepdims=True))
            shrink = jnp.exp2((resp_top - top) * power)
            weights = jnp.exp2((scores - top) * power)
            inverse = 1.0 / (shrink * stat_v[h, t, 1:2] + jnp.sum(weights, 0, keepdims=True))
            factor = shrink * inverse
            prob = weights * inverse
            delta = factor * stat_v[h, t, 2:3] + jnp.sum(prob * dprob, 0, keepdims=True)
            dscore = (prob * (dprob - delta)).astype(jnp.bfloat16)
            dfront_v[h, t] = dscore
            stat_v[h, t, 3:4] = factor
            stat_v[h, t, 4:5] = delta
            front_value += dot(prob.astype(jnp.bfloat16), grad, NN)
            front_key += dot(dscore, query, NN)
        send_part(i, front_key * SCALE, front_value)

    def send_part(i, front_key, front_value):
        h = order[i]
        for q in range(n_p):
            part_send[i, q] = jnp.concatenate(
                [front_key[q * own:(q + 1) * own], front_value[q * own:(q + 1) * own]], 0
            ).astype(jnp.bfloat16)

        @pl.when(me_r != h * stride)
        def _():
            part_copy(i, 0).start()

        @pl.when(me_r == h * stride)
        def _():
            part_recv[me] = part_send[i, me_p]

        for step in range(1, n_p):
            part_copy(i, step).start()

    def total_copy(i, step):
        return pltpu.make_async_remote_copy(
            src_ref=total_v.at[i], dst_ref=total_v.at[i],
            send_sem=total_ssem.at[step], recv_sem=total_rsem.at[i],
            device_id=(me_p, peers_r[step]), device_id_type=MESH)

    def add_up(i):
        @pl.when(me_r == order[i] * stride)
        def _():
            others = part_recv.at[pl.ds(0, n_dev - 1)]
            pltpu.make_async_copy(others, others, part_rsem).wait()

            def body(s, totals):
                prompt = group_ref[s]
                piece = part_recv[s].astype(jnp.float32)
                return tuple(
                    total + jnp.where(prompt == p, piece, 0.0) for p, total in enumerate(totals))

            zero = jnp.zeros(part_recv.shape[1:], jnp.float32)
            totals = lax.fori_loop(0, n_dev, body, (zero,) * prompts)
            for p in range(prompts):
                total_v[i, p] = totals[p].astype(jnp.bfloat16)
            for step in range(1, n_r):
                total_copy(i, step).start()

    stores = []

    def store(ref, out):
        copy = pltpu.make_async_copy(ref, out, store_sem.at[len(stores)])
        copy.start()
        stores.append(copy)

    def put_dquery(h, t, turned):
        turned = (turned * SCALE).astype(jnp.bfloat16)
        for g in range(GROUP):
            dquery_v[t * TILE:(t + 1) * TILE, (h * GROUP + g) * HD:(h * GROUP + g + 1) * HD] = (
                turned[:, g * TILE:(g + 1) * TILE].T)

    def resp_terms(i):
        h = order[i]
        lanes = lanes_of(h)
        key_sums, value_sums = [], []
        for t in range(tiles):
            depth = (t + 1) * TILE
            query = stacked(query_v, h, t)
            prob = weight_v[h, t, 0:depth] * stat_v[h, t, 3:4]
            dscore = (prob * (dprob_v[h, t, 0:depth] - stat_v[h, t, 4:5])).astype(jnp.bfloat16)
            value_sums.append(dot(prob.astype(jnp.bfloat16), live_grad_v[h, t], NN))
            key_sums.append(dot(dscore, query, NN))
            put_dquery(h, t, dot(
                keys_v[0:front + depth, lanes],
                jnp.concatenate([dfront_v[h, t], dscore], 0), TN))
        for t in range(tiles):
            span = slice(t * TILE, (t + 1) * TILE)
            dkey_v[span, lanes] = (
                sum(s[span] for s in key_sums[t:]) * SCALE).astype(jnp.bfloat16)
            dvalue_v[span, lanes] = sum(s[span] for s in value_sums[t:]).astype(jnp.bfloat16)
        cols = pl.ds(h * wide, wide)
        store(dquery_v.at[:, cols], dquery_hbm.at[0, :, cols])

    def whole_scores(i):
        h = order[i]
        lanes = lanes_of(h)
        loads["q", h].wait()
        loads["g", h].wait()
        key_sums, value_sums = [], []
        for t in range(tiles):
            depth = front + (t + 1) * TILE
            query = stacked(query_v, h, t)
            grad = stacked(grad_v, h, t) * jnp.concatenate(
                [live[t * TILE:(t + 1) * TILE]] * GROUP, 0)
            scores = dot(keys_v[0:depth, lanes], query, NT)
            scores = jnp.concatenate(
                [scores[:depth - TILE],
                 scores[depth - TILE:] + jnp.concatenate([bias_v[...]] * GROUP, 1)], 0)
            top = jnp.max(scores, 0, keepdims=True)
            weights = jnp.exp2((scores - top) * power)
            prob = weights * (1.0 / jnp.sum(weights, 0, keepdims=True))
            dprob = dot(values_v[0:depth, lanes], grad, NT)
            delta = jnp.sum(prob * dprob, 0, keepdims=True)
            dscore = (prob * (dprob - delta)).astype(jnp.bfloat16)
            dscore_v[i - EARLY, t, 0:depth] = dscore
            value_sums.append(dot(prob.astype(jnp.bfloat16), grad, NN))
            key_sums.append(dot(dscore, query, NN))
        send_part(i, sum(s[:front] for s in key_sums) * SCALE, sum(s[:front] for s in value_sums))
        for t in range(tiles):
            span = slice(t * TILE, (t + 1) * TILE)
            low = front + t * TILE
            dkey_v[span, lanes] = (
                sum(s[low:low + TILE] for s in key_sums[t:]) * SCALE).astype(jnp.bfloat16)
            dvalue_v[span, lanes] = sum(
                s[low:low + TILE] for s in value_sums[t:]).astype(jnp.bfloat16)

    def whole_terms(i):
        h = order[i]
        for t in range(tiles):
            depth = front + (t + 1) * TILE
            put_dquery(h, t, dot(
                keys_v[0:depth, lanes_of(h)], dscore_v[i - EARLY, t, 0:depth], TN))
        cols = pl.ds(h * wide, wide)
        store(dquery_v.at[:, cols], dquery_hbm.at[0, :, cols])

    loads["k"].wait()
    loads["v"].wait()
    resp_scores(0)

    loads["pk"].wait()
    loads["pv"].wait()

    def front_of(q):
        prompt = group_ref[q * n_r + me_r]
        return jnp.concatenate(
            [pkeys_v[prompt].astype(jnp.float32), pvalues_v[prompt].astype(jnp.float32)], 0
        ).astype(jnp.bfloat16)

    for q in range(n_p):
        front_send[q] = front_of(q)
    front_recv[me_p] = front_of(me_p)
    pl.semaphore_wait(barrier, n_dev - 1)

    front_copies = []
    for step in range(1, n_p):
        to = peers_p[step]
        copy = pltpu.make_async_remote_copy(
            src_ref=front_send.at[to], dst_ref=front_recv.at[me_p],
            send_sem=front_ssem.at[step], recv_sem=front_rsem.at[me_p],
            device_id=(to, me_r), device_id_type=MESH)
        copy.start()
        front_copies.append(copy)

    resp_scores(1)

    for step in range(1, n_p):
        source = peers_p[step]
        pltpu.make_async_remote_copy(
            src_ref=front_send.at[source], dst_ref=front_recv.at[source],
            send_sem=front_ssem.at[step], recv_sem=front_rsem.at[source],
            device_id=(source, me_r), device_id_type=MESH).wait_recv()
    arrived = [front_recv[q].astype(jnp.float32) for q in range(n_p)]
    keys_v[0:front] = jnp.concatenate([a[0:own] for a in arrived], 0).astype(jnp.bfloat16)
    values_v[0:front] = jnp.concatenate([a[own:] for a in arrived], 0).astype(jnp.bfloat16)

    front_terms(0)
    front_terms(1)
    whole_scores(2)
    whole_scores(3)
    add_up(0)
    add_up(1)
    resp_terms(0)
    add_up(2)
    add_up(3)
    resp_terms(1)
    whole_terms(2)
    whole_terms(3)
    store(dkey_v, dkey_hbm.at[0])
    store(dvalue_v, dvalue_hbm.at[0])

    for i, h in enumerate(order):
        @pl.when(me_r != h * stride)
        def _():
            total_copy(i, 1).wait_recv()

        total_ref[h] = total_v[i]

    for copy in stores:
        copy.wait()
    for copy in front_copies:
        copy.wait_send()
    for i, h in enumerate(order):
        @pl.when(me_r != h * stride)
        def _():
            part_copy(i, 0).wait_send()

        for step in range(1, n_p):
            part_copy(i, step).wait_send()

        @pl.when(me_r == h * stride)
        def _():
            for step in range(1, n_r):
                total_copy(i, step).wait_send()


def write_out(dquery, dkey, dvalue, total, dquery_out, dkey_out, dvalue_out, dpkey, dpvalue, sem):
    copies = []
    cut = dquery.shape[1] // PIECES
    spans = [(dquery, dquery_out, pl.ds(n * cut, cut)) for n in range(PIECES)]
    spans.append((dkey, dkey_out, pl.ds(0, dkey.shape[1])))
    spans.append((dvalue, dvalue_out, pl.ds(0, dvalue.shape[1])))
    for n, (src, dst, rows) in enumerate(spans):
        copies.append(pltpu.make_async_copy(src.at[0, rows], dst.at[0, rows], sem.at[n]))
        copies[-1].start()
    own = dpkey.shape[1]
    for h in range(KVH):
        both = total[h].astype(jnp.float32)
        dpkey[:, :, h * HD:(h + 1) * HD] = both[:, 0:own]
        dpvalue[:, :, h * HD:(h + 1) * HD] = both[:, own:]
    for copy in copies:
        copy.wait()


def shards(n_p, n_r, query, resp_keys, resp_values, prompt_keys, prompt_values, out_grad, group, lengths):
    rows = query.shape[1]
    prompts, own, kvw = prompt_keys.shape
    front = own * n_p
    n_dev = n_p * n_r
    tiles = rows // TILE
    order = (0, 3, 1, 2)
    low = jnp.bfloat16
    vmem = pl.BlockSpec(memory_space=pltpu.VMEM)
    smem = pl.BlockSpec(memory_space=pltpu.SMEM)
    some = pl.BlockSpec(memory_space=pl.ANY)
    hbm = pl.BlockSpec(memory_space=pltpu.HBM)
    dma = pltpu.SemaphoreType.DMA
    like = lambda x, dtype: jax.ShapeDtypeStruct(x.shape, dtype)
    dquery, dkey, dvalue, total = pl.pallas_call(
        functools.partial(kernel, n_p, n_r, order),
        out_shape=(
            pltpu.VMEM(query.shape, low), pltpu.VMEM(resp_keys.shape, low),
            pltpu.VMEM(resp_values.shape, low), pltpu.VMEM((KVH, prompts, 2 * own, HD), low),
        ),
        in_specs=[smem, smem] + [hbm] * 6,
        out_specs=(some, some, some, vmem),
        scratch_shapes=[
            pltpu.VMEM((rows, QH * HD), low),
            pltpu.VMEM((rows, QH * HD), low),
            pltpu.VMEM((KVH, tiles, GROUP * TILE, HD), low),
            pltpu.VMEM((front + rows, kvw), low),
            pltpu.VMEM((front + rows, kvw), low),
            pltpu.VMEM((prompts, own, kvw), low),
            pltpu.VMEM((prompts, own, kvw), low),
            pltpu.VMEM((TILE, TILE), jnp.float32),
            pltpu.VMEM((KVH, tiles, rows, GROUP * TILE), jnp.float32),
            pltpu.VMEM((KVH, tiles, rows, GROUP * TILE), jnp.float32),
            pltpu.VMEM((KVH, tiles, 8, GROUP * TILE), jnp.float32),
            pltpu.VMEM((KVH, tiles, front, GROUP * TILE), low),
            pltpu.VMEM((KVH - EARLY, tiles, front + rows, GROUP * TILE), low),
            pltpu.VMEM((rows, QH * HD), low),
            pltpu.VMEM((rows, kvw), low),
            pltpu.VMEM((rows, kvw), low),
            pltpu.VMEM((n_p, 2 * own, kvw), low),
            pltpu.VMEM((n_p, 2 * own, kvw), low),
            pltpu.VMEM((KVH, n_p, 2 * own, HD), low),
            pltpu.VMEM((n_dev, 2 * own, HD), low),
            pltpu.VMEM((KVH, prompts, 2 * own, HD), low),
            dma((5 + 2 * KVH,)),
            dma((2 + KVH,)),
            dma((n_p,)),
            dma((n_p,)),
            dma((KVH, n_p)),
            dma,
            dma((n_r,)),
            dma((KVH,)),
        ],
        compiler_params=pltpu.CompilerParams(
            collective_id=0, has_side_effects=True, vmem_limit_bytes=60 * 1024 * 1024),
    )(group, lengths, query, out_grad, resp_keys, resp_values, prompt_keys, prompt_values)
    return pl.pallas_call(
        write_out,
        out_shape=(
            like(query, low), like(resp_keys, low), like(resp_values, low),
            like(prompt_keys, jnp.float32), like(prompt_values, jnp.float32),
        ),
        in_specs=[some, some, some, vmem],
        out_specs=(some, some, some, vmem, vmem),
        scratch_shapes=[dma((2 + PIECES,))],
        compiler_params=pltpu.CompilerParams(vmem_limit_bytes=16 * 1024 * 1024),
    )(dquery, dkey, dvalue, total)


def solution(mesh):
    return jax.shard_map(
        functools.partial(shards, mesh.shape["prompt"], mesh.shape["resp"]),
        mesh=mesh,
        in_specs=(
            P(("prompt", "resp"), None, None),
            P(("prompt", "resp"), None, None),
            P(("prompt", "resp"), None, None),
            P(None, "prompt", None),
            P(None, "prompt", None),
            P(("prompt", "resp"), None, None),
            P(),
            P(("prompt", "resp")),
        ),
        out_specs=(
            P(("prompt", "resp"), None, None),
            P(("prompt", "resp"), None, None),
            P(("prompt", "resp"), None, None),
            P(None, "prompt", None),
            P(None, "prompt", None),
        ),
        check_vma=False,
    )
```
